256 devices in a mesh: row: 32 (over x_hi, z, core), blk: 8 (over y, x_lo).
Axes of the slice: x: 4 (x_hi: 2, x_lo: 2; x = x_hi * 2 + x_lo), y: 4, z: 8, core: 2. Of those that a mesh axis runs over, the one named last changes fastest.
Arguments:
- features: bfloat16 [98304, 256], P(('row', 'blk')), may hold values from -6 to 6
- adj_tiles: bfloat16 [32, 2304, 128, 128], P('row', 'blk'), may hold values from -0.15625 to 0.15625
- tile_row: int32 [32, 2304], P('row', 'blk'), may hold values from 0 to 23, as said below
- tile_col: int32 [32, 2304], P('row', 'blk'), may hold values from 0 to 96, as said below
- weight: bfloat16 [256, 256], replicated, may hold values from -0.375 to 0.375
- bias_vec: float32 [256], replicated, may hold values from -3 to 3
- cotangent: bfloat16 [98304, 256], P(('row', 'blk')), may hold values from -6 to 6
Outputs:
- activated: bfloat16 [98304, 256], P(('row', 'blk'))
- grad_x: bfloat16 [98304, 256], P(('row', 'blk'))
- grad_w: float32 [256, 256], replicated
- grad_b: float32 [256], replicated
The draws below stay inside these ranges and needn't reach their ends.
Inputs may be any that keep to these rules, and one draw needn't show every extreme that they name: On each device the 288 slots of tile_col are non-decreasing; live slots hold 0 to 95 and come first, dead slots hold 96; live (tile_row, tile_col) pairs on one device are distinct; a device has 72 to 288 live slots, and at least one device has 288. `tile_row`: dead slots hold 0.
All inputs are finite; a program needn't handle non-finite values.
Results may differ from the reference program's by a relative error of at most 0.0075.
Values may be sent and summed in bfloat16 or wider, within the bound.
No kernel may reach another device: no remote copies, remote signals or barrier semaphores. Data moves between devices by JAX's collectives and lax.ppermute only.
A program may use at most 128 MiB of HBM per device.

```python
import jax
import jax.numpy as jnp
from jax import lax

HIDDEN_SIZE = 256
TILE = 128
NB = 384
NODES = 98304
TR = 24
TC = 96
K = 288
N_ROW = 32
N_BLK = 8


def tile_layout(key):
    slot_rows = N_BLK * NB // TILE
    slot_cols = N_ROW * NB // TILE
    slot_count = slot_rows * slot_cols
    devices = jnp.arange(N_ROW * N_BLK, dtype=jnp.int32)

    def per_device(device):
        dev_key = jax.random.fold_in(key, device)
        shuffled = jax.random.permutation(jax.random.fold_in(dev_key, 1), slot_count)[:K].astype(jnp.int32)
        live_count = jax.random.randint(jax.random.fold_in(dev_key, 2), (), K // 4, K // 2 + 1, dtype=jnp.int32)
        return (shuffled, live_count)
    shuffled, live_count = jax.vmap(per_device)(devices)
    crowded = jax.random.randint(jax.random.fold_in(key, 3), (N_ROW * N_BLK,), 0, 8, dtype=jnp.int32) == 0
    chosen = jax.random.randint(jax.random.fold_in(key, 4), (), 0, N_ROW * N_BLK, dtype=jnp.int32)
    crowded = crowded | (devices == chosen)
    live_count = jnp.where(crowded, K, live_count)
    slot_ids = jnp.where(jnp.arange(K, dtype=jnp.int32)[None, :] < live_count[:, None], shuffled, slot_count)
    slot_ids = jnp.sort(slot_ids, axis=1)
    cols_out = (slot_ids // slot_rows).reshape(N_ROW, N_BLK * K)
    rows_out = (slot_ids % slot_rows).reshape(N_ROW, N_BLK * K)
    return (cols_out, rows_out)


def draw_tile_row(key, part):
    return tile_layout(key)[1]


def draw_tile_col(key, part):
    return tile_layout(key)[0]


def shard_levels(own_key, extent, shards, low, largest):
    loudness, own = 1.0, jax.random.fold_in(own_key, 6)
    for position, shards_of in shards:
        heights = jnp.exp(jax.random.uniform(jax.random.fold_in(own, position), (shards_of,), jnp.float32, low / len(shards), largest / len(shards)))
        loudness = loudness * jnp.repeat(heights, extent[position] // shards_of).reshape([-1 if axis == position else 1 for axis in range(len(extent))])
    return loudness


def gaussian(key, extent, scale, most, pieces=(), kind=jnp.bfloat16):
    drawn = jax.random.normal(key, extent, jnp.float32) * scale
    if len(pieces) > 0:
        drawn = shard_levels(key, extent, pieces, -0.22, 0.18) * drawn
    return jnp.clip(drawn, min=-most, max=most).astype(kind)


def setup_inputs(seed: int = 0) -> dict:
    key_list = jax.random.split(jax.random.key(seed), 8)
    features = gaussian(key_list[0], (NODES, HIDDEN_SIZE), 1.0, 6.0, ((0, 256),))
    adj_tiles = gaussian(key_list[1], (N_ROW, N_BLK * K, TILE, TILE), (K * TILE // TR) ** -0.5, 0.15625, ((0, 32), (1, 8)))
    tile_row = draw_tile_row(jax.random.fold_in(key_list[7], 71), 0)
    tile_col = draw_tile_col(jax.random.fold_in(key_list[7], 71), 0)
    weight = gaussian(key_list[4], (HIDDEN_SIZE, HIDDEN_SIZE), HIDDEN_SIZE ** -0.5, 0.375)
    bias_vec = gaussian(key_list[5], (HIDDEN_SIZE,), 0.5, 3.0, (), jnp.float32)
    cotangent = gaussian(key_list[6], (NODES, HIDDEN_SIZE), 1.0, 6.0, ((0, 256),))
    return {"features": features, "adj_tiles": adj_tiles, "tile_row": tile_row, "tile_col": tile_col, "weight": weight, "bias_vec": bias_vec, "cotangent": cotangent}


def gelu_pair(pre_act, cot):
    value_out, pullback = jax.vjp(lambda v: jax.nn.gelu(v, approximate=True), pre_act)
    return (value_out, pullback(cot)[0])

def forward_slab(tile_vals, rows_in, cols_in, col_slab):
    active = (cols_in < TC).astype(jnp.float32)
    picked = col_slab[jnp.minimum(cols_in, TC - 1)].astype(jnp.float32)
    contrib = jnp.einsum('kij,kjf->kif', tile_vals.astype(jnp.float32), picked) * active[:, None, None]
    onehot = (rows_in[None, :] == jnp.arange(TR, dtype=jnp.int32)[:, None]).astype(jnp.float32)
    return jnp.einsum('rk,kif->rif', onehot, contrib, precision=lax.Precision.HIGHEST)

def backward_slab(tile_vals, rows_in, cols_in, err_slab):
    picked = err_slab[rows_in].astype(jnp.float32)
    contrib = jnp.einsum('kji,kjf->kif', tile_vals.astype(jnp.float32), picked)
    onehot = (cols_in[None, :] == jnp.arange(TC, dtype=jnp.int32)[:, None]).astype(jnp.float32)
    return jnp.einsum('ck,kif->cif', onehot, contrib, precision=lax.Precision.HIGHEST)

def reference(features, adj_tiles, tile_row, tile_col, weight, bias_vec, cotangent):
    tile_sets = adj_tiles.reshape(N_ROW, N_BLK, K, TILE, TILE)
    row_sets = tile_row.reshape(N_ROW, N_BLK, K)
    col_sets = tile_col.reshape(N_ROW, N_BLK, K)
    node_blocks = features.reshape(N_ROW, N_BLK, NB // TILE, TILE, HIDDEN_SIZE)

    def row_forward(row_idx):
        summed = jnp.zeros((TR, TILE, HIDDEN_SIZE), jnp.float32)
        for blk_idx in range(N_BLK):
            col_slab = node_blocks[:, blk_idx].reshape(TC, TILE, HIDDEN_SIZE)
            summed = summed + forward_slab(tile_sets[row_idx, blk_idx], row_sets[row_idx, blk_idx], col_sets[row_idx, blk_idx], col_slab)
        return summed
    aggregated = lax.map(row_forward, jnp.arange(N_ROW, dtype=jnp.int32))
    aggregated = aggregated.reshape(NODES, HIDDEN_SIZE).astype(jnp.bfloat16)
    pre_act = jnp.dot(aggregated, weight, preferred_element_type=jnp.float32) + bias_vec
    value_out, dpre = gelu_pair(pre_act, cotangent.astype(jnp.float32))
    activated = value_out.astype(jnp.bfloat16)
    delta_grad = dpre.astype(jnp.bfloat16)
    grad_scale = 1.0 / jnp.sqrt(jnp.float32(NODES))
    grad_w = jnp.dot(aggregated.T, delta_grad, preferred_element_type=jnp.float32) * grad_scale
    grad_b = lax.optimization_barrier(jnp.sum(delta_grad.astype(jnp.float32), axis=0)) * grad_scale
    back_feat = jnp.dot(delta_grad, weight.T, preferred_element_type=jnp.float32).astype(jnp.bfloat16)
    err_blocks = back_feat.reshape(N_ROW, TR, TILE, HIDDEN_SIZE)

    def row_backward(running, row_idx):
        err_slab = err_blocks[row_idx]
        for blk_idx in range(N_BLK):
            part_grad = backward_slab(tile_sets[row_idx, blk_idx], row_sets[row_idx, blk_idx], col_sets[row_idx, blk_idx], err_slab)
            running = running.at[:, blk_idx].add(part_grad.reshape(N_ROW, NB, HIDDEN_SIZE))
        return (running, None)
    running = lax.scan(row_backward, jnp.zeros((N_ROW, N_BLK, NB, HIDDEN_SIZE), jnp.float32), jnp.arange(N_ROW, dtype=jnp.int32))[0]
    grad_x = running.reshape(NODES, HIDDEN_SIZE).astype(jnp.bfloat16)
    return (activated, grad_x, grad_w, grad_b)
```

```python
import functools
import math

import jax
import jax.numpy as jnp
from jax import lax
from jax.experimental import pallas as pl
from jax.experimental.pallas import tpu as pltpu
from jax.sharding import Mesh, PartitionSpec as P

XH, Z, CORE, Y, XL = 2, 8, 2, 4, 2
AXES = ("xh", "z", "core", "y", "xl")
BLK = ("y", "xl")
N_BLK = Y * XL
TILE = 128
HIDDEN = 256
PER = 3
NB = PER * TILE
TR = N_BLK * PER
TC = XH * Z * CORE * PER
K = 288
GROUP = 16
GROUPS = K // GROUP
VMEM_BYTES = 56 * 2**20
bf16 = jnp.bfloat16
f32 = jnp.float32

ANY = pl.BlockSpec(memory_space=pl.ANY)
VMEM = pl.BlockSpec(memory_space=pltpu.VMEM)


def swap(axis):
    return lambda v: lax.ppermute(v, axis, [(0, 1), (1, 0)])


def turn(v, step):
    return lax.ppermute(v, "z", [(i, (i + step) % Z) for i in range(Z)])


def fetch_group(live, adj_hbm, adj, sem, g):
    first = jnp.minimum(g * GROUP, K - GROUP)
    return pltpu.make_async_copy(adj_hbm.at[pl.ds(first, GROUP)], adj.at[g], sem.at[g])


def start_groups(live_ref, adj_hbm, adj, sem):
    live = live_ref[0]
    groups = (live + GROUP - 1) // GROUP

    def begin(g, carry):
        fetch_group(live, adj_hbm, adj, sem, g).start()
        return carry

    lax.fori_loop(0, groups, begin, 0)
    return live, groups


def forward_kernel(live_ref, row_ref, pos_ref, adj_hbm, *refs):
    pieces = refs[:-6]
    out_ref, adj, slab, acc, adj_sem, piece_sem = refs[-6:]
    copies = []
    at = 0
    for n, piece in enumerate(pieces):
        size = piece.shape[0]
        copies.append(pltpu.make_async_copy(piece, slab.at[pl.ds(at, size)], piece_sem.at[n]))
        at += size
    for copy in copies:
        copy.start()
    live, groups = start_groups(live_ref, adj_hbm, adj, adj_sem)
    acc[...] = jnp.zeros_like(acc)
    for copy in copies:
        copy.wait()

    def step(g, carry):
        fetch_group(live, adj_hbm, adj, adj_sem, g).wait()
        for u in range(GROUP):
            k = g * GROUP + u
            row = jnp.where(k < live, row_ref[k], TR)
            acc[row] += jnp.dot(adj[g, u], slab[pos_ref[k]], preferred_element_type=f32)
        return carry

    lax.fori_loop(0, groups, step, 0)
    out_ref[...] = acc[:TR].astype(bf16)


def forward_tiles(live, rows, pos, adj, pieces):
    return pl.pallas_call(
        forward_kernel,
        out_shape=jax.ShapeDtypeStruct((TR, TILE, HIDDEN), bf16),
        grid_spec=pltpu.PrefetchScalarGridSpec(
            num_scalar_prefetch=3,
            grid=(),
            in_specs=[ANY] * (1 + len(pieces)),
            out_specs=VMEM,
            scratch_shapes=[
                pltpu.VMEM((GROUPS, GROUP, TILE, TILE), bf16),
                pltpu.VMEM((TC, TILE, HIDDEN), bf16),
                pltpu.VMEM((TR + 1, TILE, HIDDEN), f32),
                pltpu.SemaphoreType.DMA((GROUPS,)),
                pltpu.SemaphoreType.DMA((len(pieces),)),
            ],
        ),
        compiler_params=pltpu.CompilerParams(vmem_limit_bytes=VMEM_BYTES),
        name="forward_tiles",
    )(live, rows, pos, adj, *pieces)


def backward_kernel(live_ref, row_ref, pos_ref, adj_hbm, err_hbm, *refs):
    outs = refs[:-5]
    adj, err, acc, adj_sem, err_sem = refs[-5:]
    err_copy = pltpu.make_async_copy(err_hbm, err, err_sem)
    err_copy.start()
    live, groups = start_groups(live_ref, adj_hbm, adj, adj_sem)
    acc[...] = jnp.zeros_like(acc)
    err_copy.wait()

    def step(g, carry):
        fetch_group(live, adj_hbm, adj, adj_sem, g).wait()
        for u in range(GROUP):
            k = g * GROUP + u
            pos = jnp.where(k < live, pos_ref[k], TC)
            acc[pos] += lax.dot_general(
                adj[g, u], err[row_ref[k]], (((0,), (0,)), ((), ())), preferred_element_type=f32
            )
        return carry

    lax.fori_loop(0, groups, step, 0)
    at = 0
    for out in outs:
        out[...] = acc[at : at + out.shape[0]].astype(bf16)
        at += out.shape[0]


def backward_tiles(live, rows, pos, adj, err, sizes):
    return pl.pallas_call(
        backward_kernel,
        out_shape=[jax.ShapeDtypeStruct((size, TILE, HIDDEN), bf16) for size in sizes],
        grid_spec=pltpu.PrefetchScalarGridSpec(
            num_scalar_prefetch=3,
            grid=(),
            in_specs=[ANY, ANY],
            out_specs=[VMEM] * len(sizes),
            scratch_shapes=[
                pltpu.VMEM((GROUPS, GROUP, TILE, TILE), bf16),
                pltpu.VMEM((TR, TILE, HIDDEN), bf16),
                pltpu.VMEM((TC + 1, TILE, HIDDEN), f32),
                pltpu.SemaphoreType.DMA((GROUPS,)),
                pltpu.SemaphoreType.DMA,
            ],
        ),
        compiler_params=pltpu.CompilerParams(vmem_limit_bytes=VMEM_BYTES),
        name="backward_tiles",
    )(live, rows, pos, adj, err)


def dense_kernel(scale, parts_ref, weight_ref, bias_ref, cot_ref, act_ref, back_ref, grad_ref):
    summed = parts_ref[0].astype(f32)
    for b in range(1, N_BLK):
        summed = summed + parts_ref[b].astype(f32)
    agg = summed.astype(bf16)
    weight = weight_ref[...]
    v = jnp.dot(agg, weight, preferred_element_type=f32) + bias_ref[...]
    c = math.sqrt(2.0 / math.pi)
    t = jnp.tanh(c * (v + 0.044715 * (v * v * v)))
    act_ref[...] = (0.5 * v * (1.0 + t)).astype(bf16)
    slope = 0.5 * (1.0 + t) + 0.5 * v * (1.0 - t * t) * (c * (1.0 + 3.0 * 0.044715 * (v * v)))
    delta = (cot_ref[...].astype(f32) * slope).astype(bf16)
    back = lax.dot_general(
        delta, weight, (((1,), (1,)), ((), ())), preferred_element_type=f32
    ).astype(bf16)
    for b in range(N_BLK):
        back_ref[b] = back
    over_nodes = (((0,), (0,)), ((), ()))
    grad_ref[:, :HIDDEN] = (
        lax.dot_general(agg, delta, over_nodes, preferred_element_type=f32) * scale
    )
    ones = jnp.ones((NB, TILE), bf16)
    grad_ref[:, HIDDEN:] = (
        lax.dot_general(delta, ones, over_nodes, preferred_element_type=f32) * scale
    )


def dense_block(parts, weight, bias, cot, scale):
    return pl.pallas_call(
        functools.partial(dense_kernel, scale),
        out_shape=[
            jax.ShapeDtypeStruct((NB, HIDDEN), bf16),
            jax.ShapeDtypeStruct((N_BLK, NB, HIDDEN), bf16),
            jax.ShapeDtypeStruct((HIDDEN, HIDDEN + TILE), f32),
        ],
        in_specs=[VMEM] * 4,
        out_specs=[VMEM] * 3,
        compiler_params=pltpu.CompilerParams(vmem_limit_bytes=VMEM_BYTES),
        name="dense_block",
    )(parts, weight, bias, cot)


def gather_pieces(own):
    both = jnp.concatenate([own, swap("xh")(own)], axis=0)
    pieces = [both]
    right = left = both
    for _ in range(3):
        right = turn(right, 1)
        left = turn(left, -1)
        pieces += [right, left]
    pieces += [turn(right[:PER], 1), turn(left[PER:], -1)]
    ordered = []
    for piece in pieces[:-2]:
        ordered += [piece, swap("core")(piece)]
    last = pieces[-2:]
    ordered += last + [swap("core")(piece) for piece in last]
    return ordered


def place_of(cols, xh, z, core):
    owner = cols // PER
    away = ((owner // CORE) % Z - z) % Z
    near = jnp.where(away <= 3, 2 * away, 15 - 2 * away)
    return near, (owner % CORE) ^ core, (owner // (CORE * Z)) ^ xh, cols % PER


def scatter_sum(sends, keep):
    received = [swap("core")(part) for part in sends]
    size = XH * PER

    def mine(near):
        here = keep[near * size : (near + 1) * size].astype(f32)
        return here + received[near].astype(f32)

    far = mine(7).astype(bf16)
    right = turn(far[:PER], 1)
    left = turn(far[PER:], -1)
    onto_right, onto_left = mine(6), mine(5)
    right = jnp.concatenate([onto_right[:PER] + right.astype(f32), onto_right[PER:]], axis=0)
    left = jnp.concatenate([onto_left[:PER], onto_left[PER:] + left.astype(f32)], axis=0)
    right = turn(right.astype(bf16), 1)
    left = turn(left.astype(bf16), -1)
    for near in (4, 2):
        right = turn((mine(near) + right.astype(f32)).astype(bf16), 1)
        left = turn((mine(near - 1) + left.astype(f32)).astype(bf16), -1)
    here = mine(0) + right.astype(f32) + left.astype(f32)
    across = swap("xh")(here[PER:].astype(bf16))
    return (here[:PER] + across.astype(f32)).astype(bf16)


def shards(features, adj_tiles, tile_row, tile_col, weight, bias_vec, cotangent):
    adj = adj_tiles[0]
    rows = tile_row[0]
    cols = tile_col[0]
    xh, z, core = (lax.axis_index(axis) for axis in ("xh", "z", "core"))
    live = jnp.sum((cols < TC).astype(jnp.int32)).reshape(1)
    near, other, across, part = place_of(jnp.minimum(cols, TC - 1), xh, z, core)
    slab_pos = ((near * CORE + other) * XH + across) * PER + part
    sum_pos = ((other * Z + near) * XH + across) * PER + part

    pieces = gather_pieces(features.reshape(PER, TILE, HIDDEN))
    partial = forward_tiles(live, rows, slab_pos, adj, pieces)
    parts = lax.all_to_all(
        partial.reshape(N_BLK, NB, HIDDEN), BLK, split_axis=0, concat_axis=0, tiled=True
    )
    scale = 1.0 / math.sqrt(NB * XH * Z * CORE * N_BLK)
    activated, back, grads = dense_block(parts, weight, bias_vec.reshape(1, HIDDEN), cotangent, scale)
    err = lax.all_to_all(back, BLK, split_axis=0, concat_axis=0, tiled=True)

    grad_rows = lax.all_to_all(grads, AXES, split_axis=0, concat_axis=0, tiled=True)
    grad_row = jnp.sum(grad_rows, axis=0, keepdims=True)
    grads = lax.all_to_all(
        jnp.broadcast_to(grad_row, grads.shape), AXES, split_axis=0, concat_axis=0, tiled=True
    )

    half = TC // CORE
    step = half // Z
    outs = backward_tiles(
        live, rows, sum_pos, adj, err.reshape(TR, TILE, HIDDEN), [half] + [step] * Z
    )
    grad_x = scatter_sum(outs[1:], outs[0])
    return (activated, grad_x.reshape(NB, HIDDEN), grads[:, :HIDDEN], grads[:, HIDDEN])


def solution(mesh):
    cut = Mesh(mesh.devices.reshape(XH, Z, CORE, Y, XL), AXES)
    row = ("xh", "z", "core")
    return jax.shard_map(
        shards,
        mesh=cut,
        in_specs=(
            P(AXES, None),
            P(row, BLK, None, None),
            P(row, BLK),
            P(row, BLK),
            P(),
            P(),
            P(AXES, None),
        ),
        out_specs=(P(AXES, None), P(AXES, None), P(), P()),
        check_vma=False,
    )
```

```python
import functools
import math

import jax
import jax.numpy as jnp
from jax import lax
from jax.experimental import pallas as pl
from jax.experimental.pallas import tpu as pltpu
from jax.sharding import Mesh, PartitionSpec as P

XH, Z, CORE, Y, XL = 2, 8, 2, 4, 2
AXES = ("xh", "z", "core", "y", "xl")
BLK = ("y", "xl")
N_BLK = Y * XL
TILE = 128
HIDDEN = 256
PER = 3
NB = PER * TILE
TR = N_BLK * PER
TC = XH * Z * CORE * PER
K = 288
SPAN = CORE * PER
SPANS = XH * Z
NEAR_TILES = CORE * XH * PER
GROUP = 8
EXTRA = 48
GRAD_ROWS = HIDDEN // N_BLK
AWAY = (0, -1, 1, -2, 2, -3, 3, 4)
VMEM_BYTES = 56 * 2**20
bf16 = jnp.bfloat16
f32 = jnp.float32

ANY = pl.BlockSpec(memory_space=pl.ANY)
HBM = pl.BlockSpec(memory_space=pltpu.HBM)
VMEM = pl.BlockSpec(memory_space=pltpu.VMEM)
SMEM = pl.BlockSpec(memory_space=pltpu.SMEM)


def swap(axis):
    return lambda v: lax.ppermute(v, axis, [(0, 1), (1, 0)])


def turn(v, step):
    return lax.ppermute(v, "z", [(i, (i + step) % Z) for i in range(Z)])


def max_groups(nears):
    return min(K // GROUP + XH * len(nears), XH * len(nears) * SPAN * TR // GROUP)


def plan_groups(starts_ref, z_ref, nears, adj_hbm, adj, sem, base_ref, first_ref, end_ref):
    count = jnp.int32(0)
    for near in nears:
        there = lax.rem(z_ref[0] + AWAY[near] + Z, Z)
        for xh in range(XH):
            low = starts_ref[xh * Z + there]
            high = starts_ref[xh * Z + there + 1]
            size = (high - low + GROUP - 1) // GROUP

            def begin(g, carry, low=low, high=high, count=count):
                first = low + g * GROUP
                base = jnp.minimum(first, K - GROUP)
                base_ref[count + g] = base
                first_ref[count + g] = first
                end_ref[count + g] = high
                pltpu.make_async_copy(
                    adj_hbm.at[pl.ds(base, GROUP)], adj.at[count + g], sem.at[count + g]
                ).start()
                return carry

            lax.fori_loop(0, size, begin, 0)
            count = count + size
    base_ref[count] = 0
    first_ref[count] = 0
    end_ref[count] = 0
    return count


def for_pairs(count, adj_hbm, adj, sem, base_ref, first_ref, end_ref, work):
    def wait(g):
        pltpu.make_async_copy(adj_hbm.at[pl.ds(0, GROUP)], adj.at[g], sem.at[g]).wait()

    def step(i, carry):
        wait(2 * i)

        @pl.when(2 * i + 1 < count)
        def _():
            wait(2 * i + 1)

        for g in (2 * i, 2 * i + 1):
            for u in range(GROUP):
                k = base_ref[g] + u
                work(g, u, k, (k >= first_ref[g]) & (k < end_ref[g]))
        return carry

    lax.fori_loop(0, (count + 1) // 2, step, 0)


def group_scratch(nears):
    groups = max_groups(nears) + 1
    return [
        pltpu.VMEM((groups, GROUP, TILE, TILE), bf16),
        pltpu.SemaphoreType.DMA((groups,)),
        pltpu.SMEM((groups,), jnp.int32),
        pltpu.SMEM((groups,), jnp.int32),
        pltpu.SMEM((groups,), jnp.int32),
    ]


def forward_kernel(
    nears, total, final, starts_ref, z_ref, row_ref, pos_ref, adj_hbm, before_hbm, *refs
):
    pieces = refs[:total]
    refs = refs[total:]
    if final:
        out_ref, slab, piece_sem, adj, adj_sem, base_ref, first_ref, end_ref, acc = refs
    else:
        acc, zero_ref, slab, piece_sem, adj, adj_sem, base_ref, first_ref, end_ref = refs
        zero_ref[0] = 0
    copies = []
    at = 0
    for n, piece in enumerate(pieces):
        size = piece.shape[0]
        copies.append(pltpu.make_async_copy(piece, slab.at[pl.ds(at, size)], piece_sem.at[n]))
        at += size
    if nears[0] > 0:
        copies.append(pltpu.make_async_copy(before_hbm, acc, piece_sem.at[total]))
    for copy in copies:
        copy.start()
    count = plan_groups(
        starts_ref, z_ref, nears, adj_hbm, adj, adj_sem, base_ref, first_ref, end_ref
    )
    if nears[0] == 0:
        acc[...] = jnp.zeros_like(acc)
    for copy in copies:
        copy.wait()

    def work(g, u, k, live):
        row = jnp.where(live, row_ref[k], TR)
        pos = jnp.where(live, pos_ref[k] - nears[0] * NEAR_TILES, 0)
        acc[row] += jnp.dot(adj[g, u], slab[pos], preferred_element_type=f32)

    for_pairs(count, adj_hbm, adj, adj_sem, base_ref, first_ref, end_ref, work)
    if final:
        out_ref[...] = acc[:TR].astype(bf16)


def tile_cost(nears):
    tiles = K * len(nears) // Z
    return pl.CostEstimate(
        flops=tiles * 2 * TILE * TILE * HIDDEN, bytes_accessed=tiles * 6 * TILE * TILE, transcendentals=0
    )


def forward_tiles(scalars, adj, before, pieces, nears, final):
    acc_shape = (TR + 1, TILE, HIDDEN)
    if before is None:
        before = scalars[0]
    if final:
        out_shape, out_specs = jax.ShapeDtypeStruct((TR, TILE, HIDDEN), bf16), VMEM
    else:
        out_shape = [jax.ShapeDtypeStruct(acc_shape, f32), jax.ShapeDtypeStruct((1,), jnp.int32)]
        out_specs = [VMEM, SMEM]
    return pl.pallas_call(
        functools.partial(forward_kernel, nears, len(pieces), final),
        out_shape=out_shape,
        grid_spec=pltpu.PrefetchScalarGridSpec(
            num_scalar_prefetch=4,
            grid=(),
            in_specs=[HBM] + [ANY] * (1 + len(pieces)),
            out_specs=out_specs,
            scratch_shapes=[
                pltpu.VMEM((len(nears) * NEAR_TILES, TILE, HIDDEN), bf16),
                pltpu.SemaphoreType.DMA((len(pieces) + 1,)),
            ]
            + group_scratch(nears)
            + ([pltpu.VMEM(acc_shape, f32)] if final else []),
        ),
        compiler_params=pltpu.CompilerParams(
            vmem_limit_bytes=VMEM_BYTES
        ),
        cost_estimate=tile_cost(nears),
        name="forward_tiles",
    )(*scalars, adj, before, *pieces)


def backward_kernel(nears, ignored, starts_ref, z_ref, row_ref, pos_ref, adj_hbm, err_hbm, *refs):
    refs = refs[ignored:]
    outs = refs[: 2 * len(nears)]
    err, err_sem, adj, adj_sem, base_ref, first_ref, end_ref, acc = refs[2 * len(nears) :]
    copies = [
        pltpu.make_async_copy(
            err_hbm.at[i // PER, pl.ds(i % PER * TILE, TILE)], err.at[i], err_sem.at[i]
        )
        for i in range(TR)
    ]
    for copy in copies:
        copy.start()
    count = plan_groups(
        starts_ref, z_ref, nears, adj_hbm, adj, adj_sem, base_ref, first_ref, end_ref
    )
    acc[...] = jnp.zeros_like(acc)
    for copy in copies:
        copy.wait()

    def work(g, u, k, live):
        pos = jnp.where(live, pos_ref[k] - nears[0] * NEAR_TILES, len(nears) * NEAR_TILES)
        acc[pos] += lax.dot_general(
            adj[g, u], err[row_ref[k]], (((0,), (0,)), ((), ())), preferred_element_type=f32
        )

    for_pairs(count, adj_hbm, adj, adj_sem, base_ref, first_ref, end_ref, work)
    for i, out in enumerate(outs):
        out[...] = acc[i * XH * PER : (i + 1) * XH * PER].astype(bf16)


def backward_tiles(scalars, adj, err, nears, after):
    return pl.pallas_call(
        functools.partial(backward_kernel, nears, len(after)),
        out_shape=[jax.ShapeDtypeStruct((XH * PER, TILE, HIDDEN), bf16)] * (2 * len(nears)),
        grid_spec=pltpu.PrefetchScalarGridSpec(
            num_scalar_prefetch=4,
            grid=(),
            in_specs=[HBM] + [ANY] * (1 + len(after)),
            out_specs=[VMEM] * (2 * len(nears)),
            scratch_shapes=[
                pltpu.VMEM((TR, TILE, HIDDEN), bf16),
                pltpu.SemaphoreType.DMA((TR,)),
            ]
            + group_scratch(nears)
            + [pltpu.VMEM((len(nears) * NEAR_TILES + 1, TILE, HIDDEN), f32)],
        ),
        compiler_params=pltpu.CompilerParams(
            vmem_limit_bytes=VMEM_BYTES
        ),
        cost_estimate=tile_cost(nears),
        name="backward_tiles",
    )(*scalars, adj, err, *after)


def dense_kernel(scale, parts_ref, weight_ref, bias_ref, cot_ref, act_ref, back_ref):
    summed = parts_ref[0].astype(f32)
    for b in range(1, N_BLK):
        summed = summed + parts_ref[b].astype(f32)
    agg = summed.astype(bf16)
    weight = weight_ref[...]
    v = jnp.dot(agg, weight, preferred_element_type=f32) + bias_ref[...]
    c = math.sqrt(2.0 / math.pi)
    t = jnp.tanh(c * (v + 0.044715 * (v * v * v)))
    act_ref[...] = (0.5 * v * (1.0 + t)).astype(bf16)
    slope = 0.5 * (1.0 + t) + 0.5 * v * (1.0 - t * t) * (c * (1.0 + 3.0 * 0.044715 * (v * v)))
    delta = (cot_ref[...].astype(f32) * slope).astype(bf16)
    back = lax.dot_general(
        delta, weight, (((1,), (1,)), ((), ())), preferred_element_type=f32
    ).astype(bf16)
    over_nodes = (((0,), (0,)), ((), ()))
    grad_w = lax.dot_general(agg, delta, over_nodes, preferred_element_type=f32) * scale
    grad_b = jnp.sum(delta.astype(f32), axis=0, keepdims=True) * scale
    grad_b = jnp.broadcast_to(grad_b, (EXTRA - GRAD_ROWS, HIDDEN)).astype(bf16)
    for b in range(N_BLK):
        back_ref[b, :NB] = back
        back_ref[b, NB : NB + GRAD_ROWS] = grad_w[b * GRAD_ROWS : (b + 1) * GRAD_ROWS].astype(bf16)
        back_ref[b, NB + GRAD_ROWS :] = grad_b


def dense_block(parts, weight, bias, cot, scale):
    return pl.pallas_call(
        functools.partial(dense_kernel, scale),
        out_shape=[
            jax.ShapeDtypeStruct((NB, HIDDEN), bf16),
            jax.ShapeDtypeStruct((N_BLK, NB + EXTRA, HIDDEN), bf16),
        ],
        in_specs=[VMEM] * 4,
        out_specs=[VMEM] * 2,
        compiler_params=pltpu.CompilerParams(vmem_limit_bytes=VMEM_BYTES),
        name="dense_block",
    )(parts, weight, bias, cot)


def by_z_kernel(z_ref, *refs):
    total_ref, rows = refs[Z:]
    for away in range(Z):
        rows[away] = refs[away][...]
    total = jnp.zeros((EXTRA, HIDDEN), f32)
    for there in range(Z):
        total += rows[lax.rem(there - z_ref[0] + Z, Z)].astype(f32)
    total_ref[...] = total


def sum_by_z(z, parts):
    return pl.pallas_call(
        by_z_kernel,
        out_shape=jax.ShapeDtypeStruct((EXTRA, HIDDEN), f32),
        grid_spec=pltpu.PrefetchScalarGridSpec(
            num_scalar_prefetch=1,
            grid=(),
            in_specs=[VMEM] * Z,
            out_specs=VMEM,
            scratch_shapes=[pltpu.VMEM((Z, EXTRA, HIDDEN), bf16)],
        ),
        compiler_params=pltpu.CompilerParams(vmem_limit_bytes=4 * 2**20),
        name="sum_by_z",
    )(z, *parts)


def gather_forward(scalars, adj, own):
    def pair(piece):
        return [piece, swap("core")(piece)]

    both = jnp.concatenate([own, swap("xh")(own)], axis=0)
    right1, left1 = turn(both, 1), turn(both, -1)
    right2, left2 = turn(right1, 1), turn(left1, -1)
    near = pair(both) + pair(right1) + pair(left1)
    partial, zero = forward_tiles(scalars, adj, None, near, (0, 1, 2), False)
    right3, left3 = turn(right2, 1), turn(left2, -1)
    last = [
        turn(lax.dynamic_slice_in_dim(right3, zero[0], PER), 1),
        turn(lax.dynamic_slice_in_dim(left3, zero[0] + PER, PER), -1),
    ]
    middle = pair(right2) + pair(left2) + pair(right3) + pair(left3)
    partial, _ = forward_tiles(scalars, adj, partial, middle, (3, 4, 5, 6), False)
    last += [swap("core")(piece) for piece in last]
    return forward_tiles(scalars, adj, partial, last, (7,), True)


def place_of(cols, xh, z, core):
    owner = cols // PER
    away = ((owner // CORE) % Z - z) % Z
    near = jnp.where(away <= 3, 2 * away, 15 - 2 * away)
    return ((near * CORE + (owner % CORE ^ core)) * XH + (owner // (CORE * Z) ^ xh)) * PER + cols % PER


def backward_scatter(scalars, adj, err, grads):
    rows = XH * NB
    sums = [None] * Z

    def tiles(nears, after):
        outs = backward_tiles(scalars, adj, err, nears, after)
        for i, near in enumerate(nears):
            keep, send = outs[2 * i], swap("core")(outs[2 * i + 1])
            sums[near] = (keep.astype(f32) + send.astype(f32)).reshape(rows, HIDDEN)

    tiles((5, 6, 7), [])
    far = sums[7].astype(bf16)
    right = jnp.concatenate([far[:NB], grads], axis=0)
    left = jnp.concatenate([far[NB:], grads], axis=0)
    from_left, from_right = [], []
    for step in range(4):
        if step == 0:
            tiles((3, 4), [right, left])
        if step == 1:
            tiles((0, 1, 2), [right, left])
        right, left = turn(right, 1), turn(left, -1)
        size = rows if step > 0 else NB
        from_left.append(right[size:])
        if step < 3:
            from_right.append(left[size:])
        right, left = right[:size].astype(f32), left[:size].astype(f32)
        if step == 0:
            right = jnp.concatenate([sums[6][:NB] + right, sums[6][NB:]], axis=0)
            left = jnp.concatenate([sums[5][:NB], sums[5][NB:] + left], axis=0)
        else:
            right = right + sums[6 - 2 * step]
            left = left + sums[5 - 2 * step] if step < 3 else left
        if step < 3:
            right = jnp.concatenate([right.astype(bf16), from_left[-1]], axis=0)
        if step < 2:
            left = jnp.concatenate([left.astype(bf16), from_right[-1]], axis=0)
        if step == 2:
            left = left.astype(bf16)
    here = right + left
    across = swap("xh")(here[NB:].astype(bf16))
    grad_x = (here[:NB] + across.astype(f32)).astype(bf16)
    return grad_x, [grads] + from_right + from_left[::-1]


def both_sides(rows, axis):
    rows = rows.astype(bf16)
    return rows.astype(f32) + swap(axis)(rows).astype(f32)


def shards(features, adj_tiles, tile_row, tile_col, weight, bias_vec, cotangent):
    adj = adj_tiles[0]
    rows = tile_row[0]
    cols = tile_col[0]
    xh, z, core = (lax.axis_index(axis) for axis in ("xh", "z", "core"))
    edges = jnp.arange(SPANS + 1, dtype=jnp.int32) * SPAN
    starts = jnp.sum((cols[None, :] < edges[:, None]).astype(jnp.int32), axis=1)
    pos = place_of(jnp.minimum(cols, TC - 1), xh, z, core)
    scalars = (starts, z.reshape(1).astype(jnp.int32), rows, pos)

    partial = gather_forward(scalars, adj, features.reshape(PER, TILE, HIDDEN))
    parts = lax.all_to_all(
        partial.reshape(N_BLK, NB, HIDDEN), BLK, split_axis=0, concat_axis=0, tiled=True
    )
    scale = 1.0 / math.sqrt(NB * XH * Z * CORE * N_BLK)
    activated, back = dense_block(parts, weight, bias_vec.reshape(1, HIDDEN), cotangent, scale)
    back = lax.all_to_all(back, BLK, split_axis=0, concat_axis=0, tiled=True)

    grads = jnp.sum(back[:, NB:].astype(f32), axis=0)
    grads = both_sides(both_sides(grads, "core"), "xh").astype(bf16)
    grad_x, by_z = backward_scatter(scalars, adj, back, grads)
    grads = sum_by_z(scalars[1], by_z)
    grad_w = lax.all_to_all(
        jnp.tile(grads[:GRAD_ROWS], (N_BLK, 1)), BLK, split_axis=0, concat_axis=0, tiled=True
    )
    return (activated, grad_x, grad_w, grads[GRAD_ROWS])


def solution(mesh):
    cut = Mesh(mesh.devices.reshape(XH, Z, CORE, Y, XL), AXES)
    row = ("xh", "z", "core")
    return jax.shard_map(
        shards,
        mesh=cut,
        in_specs=(
            P(AXES, None),
            P(row, BLK, None, None),
            P(row, BLK),
            P(row, BLK),
            P(),
            P(),
            P(AXES, None),
        ),
        out_specs=(P(AXES, None), P(AXES, None), P(), P()),
        check_vma=False,
    )
```

```python
import functools
import math

import jax
import jax.numpy as jnp
from jax import lax
from jax.experimental import pallas as pl
from jax.experimental.pallas import tpu as pltpu
from jax.sharding import Mesh, PartitionSpec as P

XH, Z, CORE, Y, XL = 2, 8, 2, 4, 2
AXES = ("xh", "z", "core", "y", "xl")
BLK = ("y", "xl")
N_BLK = Y * XL
TILE = 128
HIDDEN = 256
PER = 3
NB = PER * TILE
TR = N_BLK * PER
TC = XH * Z * CORE * PER
K = 288
SPAN = CORE * PER
SPANS = XH * Z
NEAR_TILES = CORE * XH * PER
GROUP = 8
EXTRA = 48
GRAD_ROWS = HIDDEN // N_BLK
AWAY = (0, -1, 1, -2, 2, -3, 3, 4)
VMEM_BYTES = 56 * 2**20
bf16 = jnp.bfloat16
f32 = jnp.float32

ANY = pl.BlockSpec(memory_space=pl.ANY)
HBM = pl.BlockSpec(memory_space=pltpu.HBM)
VMEM = pl.BlockSpec(memory_space=pltpu.VMEM)
SMEM = pl.BlockSpec(memory_space=pltpu.SMEM)


def swap(axis):
    return lambda v: lax.ppermute(v, axis, [(0, 1), (1, 0)])


def turn(v, step):
    return lax.ppermute(v, "z", [(i, (i + step) % Z) for i in range(Z)])


def max_groups(nears):
    return min(K // GROUP + XH * len(nears), XH * len(nears) * SPAN * TR // GROUP)


def plan_groups(starts_ref, z_ref, nears, adj_hbm, adj, sem, base_ref, first_ref, end_ref):
    count = jnp.int32(0)
    for near in nears:
        there = lax.rem(z_ref[0] + AWAY[near] + Z, Z)
        for xh in range(XH):
            low = starts_ref[xh * Z + there]
            high = starts_ref[xh * Z + there + 1]
            size = (high - low + GROUP - 1) // GROUP

            def begin(g, carry, low=low, high=high, count=count):
                first = low + g * GROUP
                base = jnp.minimum(first, K - GROUP)
                base_ref[count + g] = base
                first_ref[count + g] = first
                end_ref[count + g] = high
                pltpu.make_async_copy(
                    adj_hbm.at[pl.ds(base, GROUP)], adj.at[count + g], sem.at[count + g]
                ).start()
                return carry

            lax.fori_loop(0, size, begin, 0)
            count = count + size
    base_ref[count] = 0
    first_ref[count] = 0
    end_ref[count] = 0
    return count


def for_pairs(count, adj_hbm, adj, sem, base_ref, first_ref, end_ref, work):
    def wait(g):
        pltpu.make_async_copy(adj_hbm.at[pl.ds(0, GROUP)], adj.at[g], sem.at[g]).wait()

    def step(i, carry):
        wait(2 * i)

        @pl.when(2 * i + 1 < count)
        def _():
            wait(2 * i + 1)

        for g in (2 * i, 2 * i + 1):
            for u in range(GROUP):
                k = base_ref[g] + u
                work(g, u, k, (k >= first_ref[g]) & (k < end_ref[g]))
        return carry

    lax.fori_loop(0, (count + 1) // 2, step, 0)


def group_scratch(nears):
    groups = max_groups(nears) + 1
    return [
        pltpu.VMEM((groups, GROUP, TILE, TILE), bf16),
        pltpu.SemaphoreType.DMA((groups,)),
        pltpu.SMEM((groups,), jnp.int32),
        pltpu.SMEM((groups,), jnp.int32),
        pltpu.SMEM((groups,), jnp.int32),
    ]


def forward_kernel(
    nears, total, final, starts_ref, z_ref, row_ref, pos_ref, adj_hbm, before_hbm, *refs
):
    pieces = refs[:total]
    refs = refs[total:]
    if final:
        out_ref, slab, piece_sem, adj, adj_sem, base_ref, first_ref, end_ref, acc = refs
    else:
        acc, zero_ref, slab, piece_sem, adj, adj_sem, base_ref, first_ref, end_ref = refs
        zero_ref[0] = 0
    copies = []
    at = 0
    for n, piece in enumerate(pieces):
        size = piece.shape[0]
        copies.append(pltpu.make_async_copy(piece, slab.at[pl.ds(at, size)], piece_sem.at[n]))
        at += size
    if nears[0] > 0:
        copies.append(pltpu.make_async_copy(before_hbm, acc, piece_sem.at[total]))
    for copy in copies:
        copy.start()
    count = plan_groups(
        starts_ref, z_ref, nears, adj_hbm, adj, adj_sem, base_ref, first_ref, end_ref
    )
    if nears[0] == 0:
        acc[...] = jnp.zeros_like(acc)
    for copy in copies:
        copy.wait()

    def work(g, u, k, live):
        row = jnp.where(live, row_ref[k], TR)
        pos = jnp.where(live, pos_ref[k] - nears[0] * NEAR_TILES, 0)
        acc[row] += jnp.dot(adj[g, u], slab[pos], preferred_element_type=f32)

    for_pairs(count, adj_hbm, adj, adj_sem, base_ref, first_ref, end_ref, work)
    if final:
        out_ref[...] = acc[:TR].astype(bf16)


def tile_cost(nears):
    tiles = K * len(nears) // Z
    return pl.CostEstimate(
        flops=tiles * 2 * TILE * TILE * HIDDEN, bytes_accessed=tiles * 6 * TILE * TILE, transcendentals=0
    )


def forward_tiles(scalars, adj, before, pieces, nears, final):
    acc_shape = (TR + 1, TILE, HIDDEN)
    if before is None:
        before = scalars[0]
    if final:
        out_shape, out_specs = jax.ShapeDtypeStruct((TR, TILE, HIDDEN), bf16), VMEM
    else:
        out_shape = [jax.ShapeDtypeStruct(acc_shape, f32), jax.ShapeDtypeStruct((1,), jnp.int32)]
        out_specs = [VMEM, SMEM]
    return pl.pallas_call(
        functools.partial(forward_kernel, nears, len(pieces), final),
        out_shape=out_shape,
        grid_spec=pltpu.PrefetchScalarGridSpec(
            num_scalar_prefetch=4,
            grid=(),
            in_specs=[HBM] + [ANY] * (1 + len(pieces)),
            out_specs=out_specs,
            scratch_shapes=[
                pltpu.VMEM((len(nears) * NEAR_TILES, TILE, HIDDEN), bf16),
                pltpu.SemaphoreType.DMA((len(pieces) + 1,)),
            ]
            + group_scratch(nears)
            + ([pltpu.VMEM(acc_shape, f32)] if final else []),
        ),
        compiler_params=pltpu.CompilerParams(
            vmem_limit_bytes=VMEM_BYTES
        ),
        cost_estimate=tile_cost(nears),
        name="forward_tiles",
    )(*scalars, adj, before, *pieces)


def backward_kernel(nears, ignored, with_grads, starts_ref, z_ref, row_ref, pos_ref, adj_hbm, err_hbm, *refs):
    refs = refs[ignored:]
    outs = refs[: 2 * len(nears)]
    refs = refs[2 * len(nears) :]
    if with_grads:
        grad_ref, extra, extra_sem = refs[0], *refs[-2:]
        refs = refs[1:-2]
        extra_copy = pltpu.make_async_copy(err_hbm.at[:, pl.ds(NB, EXTRA)], extra, extra_sem)
        extra_copy.start()
    err, err_sem, adj, adj_sem, base_ref, first_ref, end_ref, acc = refs
    copies = [
        pltpu.make_async_copy(
            err_hbm.at[i // PER, pl.ds(i % PER * TILE, TILE)], err.at[i], err_sem.at[i]
        )
        for i in range(TR)
    ]
    for copy in copies:
        copy.start()
    count = plan_groups(
        starts_ref, z_ref, nears, adj_hbm, adj, adj_sem, base_ref, first_ref, end_ref
    )
    acc[...] = jnp.zeros_like(acc)
    for copy in copies:
        copy.wait()

    def work(g, u, k, live):
        pos = jnp.where(live, pos_ref[k] - nears[0] * NEAR_TILES, len(nears) * NEAR_TILES)
        acc[pos] += lax.dot_general(
            adj[g, u], err[row_ref[k]], (((0,), (0,)), ((), ())), preferred_element_type=f32
        )

    for_pairs(count, adj_hbm, adj, adj_sem, base_ref, first_ref, end_ref, work)
    if with_grads:
        extra_copy.wait()
        total = extra[0].astype(f32)
        for b in range(1, N_BLK):
            total += extra[b].astype(f32)
        grad_ref[...] = total.astype(bf16)
    for i, out in enumerate(outs):
        out[...] = acc[i * XH * PER : (i + 1) * XH * PER].astype(bf16)


def backward_tiles(scalars, adj, err, nears, after, with_grads):
    grad_shape = [jax.ShapeDtypeStruct((EXTRA, HIDDEN), bf16)] if with_grads else []
    grad_scratch = [pltpu.VMEM((N_BLK, EXTRA, HIDDEN), bf16), pltpu.SemaphoreType.DMA]
    return pl.pallas_call(
        functools.partial(backward_kernel, nears, len(after), with_grads),
        out_shape=[jax.ShapeDtypeStruct((XH * PER, TILE, HIDDEN), bf16)] * (2 * len(nears))
        + grad_shape,
        grid_spec=pltpu.PrefetchScalarGridSpec(
            num_scalar_prefetch=4,
            grid=(),
            in_specs=[HBM] + [ANY] * (1 + len(after)),
            out_specs=[VMEM] * (2 * len(nears) + len(grad_shape)),
            scratch_shapes=[
                pltpu.VMEM((TR, TILE, HIDDEN), bf16),
                pltpu.SemaphoreType.DMA((TR,)),
            ]
            + group_scratch(nears)
            + [pltpu.VMEM((len(nears) * NEAR_TILES + 1, TILE, HIDDEN), f32)]
            + (grad_scratch if with_grads else []),
        ),
        compiler_params=pltpu.CompilerParams(
            vmem_limit_bytes=VMEM_BYTES
        ),
        cost_estimate=tile_cost(nears),
        name="backward_tiles",
    )(*scalars, adj, err, *after)


def dense_kernel(scale, parts_ref, weight_ref, bias_ref, cot_ref, act_ref, back_ref):
    summed = parts_ref[0].astype(f32)
    for b in range(1, N_BLK):
        summed = summed + parts_ref[b].astype(f32)
    agg = summed.astype(bf16)
    weight = weight_ref[...]
    v = jnp.dot(agg, weight, preferred_element_type=f32) + bias_ref[...]
    c = math.sqrt(2.0 / math.pi)
    t = jnp.tanh(c * (v + 0.044715 * (v * v * v)))
    act_ref[...] = (0.5 * v * (1.0 + t)).astype(bf16)
    slope = 0.5 * (1.0 + t) + 0.5 * v * (1.0 - t * t) * (c * (1.0 + 3.0 * 0.044715 * (v * v)))
    delta = (cot_ref[...].astype(f32) * slope).astype(bf16)
    back = lax.dot_general(
        delta, weight, (((1,), (1,)), ((), ())), preferred_element_type=f32
    ).astype(bf16)
    over_nodes = (((0,), (0,)), ((), ()))
    grad_w = lax.dot_general(agg, delta, over_nodes, preferred_element_type=f32) * scale
    grad_b = jnp.sum(delta.astype(f32), axis=0, keepdims=True) * scale
    grad_b = jnp.broadcast_to(grad_b, (EXTRA - GRAD_ROWS, HIDDEN)).astype(bf16)
    for b in range(N_BLK):
        back_ref[b, :NB] = back
        back_ref[b, NB : NB + GRAD_ROWS] = grad_w[b * GRAD_ROWS : (b + 1) * GRAD_ROWS].astype(bf16)
        back_ref[b, NB + GRAD_ROWS :] = grad_b


def dense_block(parts, weight, bias, cot, scale):
    return pl.pallas_call(
        functools.partial(dense_kernel, scale),
        out_shape=[
            jax.ShapeDtypeStruct((NB, HIDDEN), bf16),
            jax.ShapeDtypeStruct((N_BLK, NB + EXTRA, HIDDEN), bf16),
        ],
        in_specs=[VMEM] * 4,
        out_specs=[VMEM] * 2,
        compiler_params=pltpu.CompilerParams(vmem_limit_bytes=VMEM_BYTES),
        name="dense_block",
    )(parts, weight, bias, cot)


def gather_forward(scalars, adj, own):
    def pair(piece):
        return [piece, swap("core")(piece)]

    def after(zero, one, two):
        ran = zero[0] == 0
        return jnp.where(ran, one, two), jnp.where(ran, two, one)

    both = jnp.concatenate([own, swap("xh")(own)], axis=0)
    right1, left1 = turn(both, 1), turn(both, -1)
    right2, left2 = turn(right1, 1), turn(left1, -1)
    near = pair(both) + pair(right1) + pair(left1)
    partial, zero = forward_tiles(scalars, adj, None, near, (0, 1, 2), False)
    right2, left2 = after(zero, right2, left2)
    right3, left3 = turn(right2, 1), turn(left2, -1)
    near = pair(right2) + pair(left2)
    partial, zero = forward_tiles(scalars, adj, partial, near, (3, 4), False)
    right4 = turn(lax.dynamic_slice_in_dim(right3, zero[0], PER), 1)
    left4 = turn(lax.dynamic_slice_in_dim(left3, zero[0] + PER, PER), -1)
    near = pair(right3) + pair(left3)
    partial, zero = forward_tiles(scalars, adj, partial, near, (5, 6), False)
    right4, left4 = after(zero, right4, left4)
    last = [right4, left4] + [swap("core")(piece) for piece in (right4, left4)]
    return forward_tiles(scalars, adj, partial, last, (7,), True)


def place_of(cols, xh, z, core):
    owner = cols // PER
    away = ((owner // CORE) % Z - z) % Z
    near = jnp.where(away <= 3, 2 * away, 15 - 2 * away)
    return ((near * CORE + (owner % CORE ^ core)) * XH + (owner // (CORE * Z) ^ xh)) * PER + cols % PER


def backward_scatter(scalars, adj, err):
    rows = XH * NB
    sums = [None] * Z

    def tiles(nears, after=(), with_grads=False):
        outs = backward_tiles(scalars, adj, err, nears, after, with_grads)
        for i, near in enumerate(nears):
            keep, send = outs[2 * i], swap("core")(outs[2 * i + 1])
            sums[near] = (keep.astype(f32) + send.astype(f32)).reshape(rows, HIDDEN)
        return outs[-1]

    tiles((3, 4, 5, 6, 7))
    far = sums[7].astype(bf16)
    right, left = far[:NB], far[NB:]
    right, left = turn(right, 1).astype(f32), turn(left, -1).astype(f32)
    right = jnp.concatenate([sums[6][:NB] + right, sums[6][NB:]], axis=0).astype(bf16)
    left = jnp.concatenate([sums[5][:NB], sums[5][NB:] + left], axis=0).astype(bf16)
    grads = tiles((0, 1, 2), (right, left), True)
    for near in (4, 2):
        right = (sums[near] + turn(right, 1).astype(f32)).astype(bf16)
        left = (sums[near - 1] + turn(left, -1).astype(f32)).astype(bf16)
    here = sums[0] + turn(right, 1).astype(f32) + turn(left, -1).astype(f32)
    across = swap("xh")(here[NB:].astype(bf16))
    return (here[:NB] + across.astype(f32)).astype(bf16), grads


def both_sides(rows, axis):
    rows = rows.astype(bf16)
    return rows.astype(f32) + swap(axis)(rows).astype(f32)


def shards(features, adj_tiles, tile_row, tile_col, weight, bias_vec, cotangent):
    adj = adj_tiles[0]
    rows = tile_row[0]
    cols = tile_col[0]
    xh, z, core = (lax.axis_index(axis) for axis in ("xh", "z", "core"))
    edges = jnp.arange(SPANS + 1, dtype=jnp.int32) * SPAN
    starts = jnp.sum((cols[None, :] < edges[:, None]).astype(jnp.int32), axis=1)
    pos = place_of(jnp.minimum(cols, TC - 1), xh, z, core)
    scalars = (starts, z.reshape(1).astype(jnp.int32), rows, pos)

    partial = gather_forward(scalars, adj, features.reshape(PER, TILE, HIDDEN))
    parts = lax.all_to_all(
        partial.reshape(N_BLK, NB, HIDDEN), BLK, split_axis=0, concat_axis=0, tiled=True
    )
    scale = 1.0 / math.sqrt(NB * XH * Z * CORE * N_BLK)
    activated, back = dense_block(parts, weight, bias_vec.reshape(1, HIDDEN), cotangent, scale)
    back = lax.all_to_all(back, BLK, split_axis=0, concat_axis=0, tiled=True)

    grad_x, grads = backward_scatter(scalars, adj, back)
    grads = both_sides(both_sides(grads, "core"), "xh").astype(bf16)
    by_z = lax.all_to_all(jnp.tile(grads, (Z, 1)), "z", split_axis=0, concat_axis=0, tiled=True)
    grads = jnp.sum(by_z.reshape(Z, EXTRA, HIDDEN).astype(f32), axis=0)
    grad_w = lax.all_to_all(
        jnp.tile(grads[:GRAD_ROWS], (N_BLK, 1)), BLK, split_axis=0, concat_axis=0, tiled=True
    )
    return (activated, grad_x, grad_w, grads[GRAD_ROWS])


def solution(mesh):
    cut = Mesh(mesh.devices.reshape(XH, Z, CORE, Y, XL), AXES)
    row = ("xh", "z", "core")
    return jax.shard_map(
        shards,
        mesh=cut,
        in_specs=(
            P(AXES, None),
            P(row, BLK, None, None),
            P(row, BLK),
            P(row, BLK),
            P(),
            P(),
            P(AXES, None),
        ),
        out_specs=(P(AXES, None), P(AXES, None), P(), P()),
        check_vma=False,
    )
```

```python
import functools
import math

import jax
import jax.numpy as jnp
from jax import lax
from jax.experimental import pallas as pl
from jax.experimental.pallas import tpu as pltpu
from jax.sharding import Mesh, PartitionSpec as P

XH, Z, CORE, Y, XL = 2, 8, 2, 4, 2
AXES = ("xh", "z", "core", "y", "xl")
BLK = ("y", "xl")
N_BLK = Y * XL
TILE = 128
HIDDEN = 256
PER = 3
NB = PER * TILE
TR = N_BLK * PER
TC = XH * Z * CORE * PER
K = 288
SPAN = CORE * PER
SPANS = XH * Z
NEAR_TILES = CORE * XH * PER
GROUP = 8
EXTRA = 48
GRAD_ROWS = HIDDEN // N_BLK
AWAY = (0, -1, 1, -2, 2, -3, 3, 4)
VMEM_BYTES = 56 * 2**20
bf16 = jnp.bfloat16
f32 = jnp.float32

ANY = pl.BlockSpec(memory_space=pl.ANY)
HBM = pl.BlockSpec(memory_space=pltpu.HBM)
VMEM = pl.BlockSpec(memory_space=pltpu.VMEM)
SMEM = pl.BlockSpec(memory_space=pltpu.SMEM)


def swap(axis):
    return lambda v: lax.ppermute(v, axis, [(0, 1), (1, 0)])


def turn(v, step):
    return lax.ppermute(v, "z", [(i, (i + step) % Z) for i in range(Z)])


def max_groups(nears):
    return min(K // GROUP + XH * len(nears), XH * len(nears) * SPAN * TR // GROUP)


def plan_groups(starts_ref, z_ref, nears, adj_hbm, adj, sem, base_ref, first_ref, end_ref):
    count = jnp.int32(0)
    for near in nears:
        there = lax.rem(z_ref[0] + AWAY[near] + Z, Z)
        for xh in range(XH):
            low = starts_ref[xh * Z + there]
            high = starts_ref[xh * Z + there + 1]
            size = (high - low + GROUP - 1) // GROUP

            def begin(g, carry, low=low, high=high, count=count):
                first = low + g * GROUP
                base = jnp.minimum(first, K - GROUP)
                base_ref[count + g] = base
                first_ref[count + g] = first
                end_ref[count + g] = high
                pltpu.make_async_copy(
                    adj_hbm.at[pl.ds(base, GROUP)], adj.at[count + g], sem.at[count + g]
                ).start()
                return carry

            lax.fori_loop(0, size, begin, 0)
            count = count + size
    base_ref[count] = 0
    first_ref[count] = 0
    end_ref[count] = 0
    return count


def for_pairs(count, adj_hbm, adj, sem, base_ref, first_ref, end_ref, work):
    def wait(g):
        pltpu.make_async_copy(adj_hbm.at[pl.ds(0, GROUP)], adj.at[g], sem.at[g]).wait()

    def step(i, carry):
        wait(2 * i)

        @pl.when(2 * i + 1 < count)
        def _():
            wait(2 * i + 1)

        for g in (2 * i, 2 * i + 1):
            for u in range(GROUP):
                k = base_ref[g] + u
                work(g, u, k, (k >= first_ref[g]) & (k < end_ref[g]))
        return carry

    lax.fori_loop(0, (count + 1) // 2, step, 0)


def group_scratch(nears):
    groups = max_groups(nears) + 1
    return [
        pltpu.VMEM((groups, GROUP, TILE, TILE), bf16),
        pltpu.SemaphoreType.DMA((groups,)),
        pltpu.SMEM((groups,), jnp.int32),
        pltpu.SMEM((groups,), jnp.int32),
        pltpu.SMEM((groups,), jnp.int32),
    ]


def forward_kernel(
    nears, total, final, starts_ref, z_ref, row_ref, pos_ref, adj_hbm, before_hbm, *refs
):
    pieces = refs[:total]
    refs = refs[total:]
    if final:
        out_ref, slab, piece_sem, adj, adj_sem, base_ref, first_ref, end_ref, acc = refs
    else:
        acc, zero_ref, slab, piece_sem, adj, adj_sem, base_ref, first_ref, end_ref = refs
        zero_ref[0] = 0
    copies = []
    at = 0
    for n, piece in enumerate(pieces):
        size = piece.shape[0]
        copies.append(pltpu.make_async_copy(piece, slab.at[pl.ds(at, size)], piece_sem.at[n]))
        at += size
    if nears[0] > 0:
        copies.append(pltpu.make_async_copy(before_hbm, acc, piece_sem.at[total]))
    for copy in copies:
        copy.start()
    count = plan_groups(
        starts_ref, z_ref, nears, adj_hbm, adj, adj_sem, base_ref, first_ref, end_ref
    )
    if nears[0] == 0:
        acc[...] = jnp.zeros_like(acc)
    for copy in copies:
        copy.wait()

    def work(g, u, k, live):
        row = jnp.where(live, row_ref[k], TR)
        pos = jnp.where(live, pos_ref[k] - nears[0] * NEAR_TILES, 0)
        acc[row] += jnp.dot(adj[g, u], slab[pos], preferred_element_type=f32)

    for_pairs(count, adj_hbm, adj, adj_sem, base_ref, first_ref, end_ref, work)
    if final:
        out_ref[...] = acc[:TR].astype(bf16)


def tile_cost(nears):
    tiles = K * len(nears) // Z
    return pl.CostEstimate(
        flops=tiles * 2 * TILE * TILE * HIDDEN, bytes_accessed=tiles * 6 * TILE * TILE, transcendentals=0
    )


def forward_tiles(scalars, adj, before, pieces, nears, final):
    acc_shape = (TR + 1, TILE, HIDDEN)
    if before is None:
        before = scalars[0]
    if final:
        out_shape, out_specs = jax.ShapeDtypeStruct((TR, TILE, HIDDEN), bf16), VMEM
    else:
        out_shape = [jax.ShapeDtypeStruct(acc_shape, f32), jax.ShapeDtypeStruct((1,), jnp.int32)]
        out_specs = [VMEM, SMEM]
    return pl.pallas_call(
        functools.partial(forward_kernel, nears, len(pieces), final),
        out_shape=out_shape,
        grid_spec=pltpu.PrefetchScalarGridSpec(
            num_scalar_prefetch=4,
            grid=(),
            in_specs=[HBM] + [ANY] * (1 + len(pieces)),
            out_specs=out_specs,
            scratch_shapes=[
                pltpu.VMEM((len(nears) * NEAR_TILES, TILE, HIDDEN), bf16),
                pltpu.SemaphoreType.DMA((len(pieces) + 1,)),
            ]
            + group_scratch(nears)
            + ([pltpu.VMEM(acc_shape, f32)] if final else []),
        ),
        compiler_params=pltpu.CompilerParams(
            vmem_limit_bytes=VMEM_BYTES
        ),
        cost_estimate=tile_cost(nears),
        name="forward_tiles",
    )(*scalars, adj, before, *pieces)


def backward_kernel(starts_ref, z_ref, row_ref, pos_ref, adj_hbm, err_hbm, *refs):
    nears = tuple(range(Z))
    outs = refs[: 2 * Z]
    err, err_sem, extra, extra_sem, adj, adj_sem, base_ref, first_ref, end_ref, acc = refs[2 * Z :]
    copies = [
        pltpu.make_async_copy(
            err_hbm.at[i // PER, pl.ds(i % PER * TILE, TILE)], err.at[i], err_sem.at[i]
        )
        for i in range(TR)
    ]
    copies.append(pltpu.make_async_copy(err_hbm.at[:, pl.ds(NB, EXTRA)], extra, extra_sem))
    for copy in copies:
        copy.start()
    count = plan_groups(
        starts_ref, z_ref, nears, adj_hbm, adj, adj_sem, base_ref, first_ref, end_ref
    )
    acc[...] = jnp.zeros_like(acc)
    for copy in copies:
        copy.wait()

    def work(g, u, k, live):
        pos = jnp.where(live, pos_ref[k], TC)
        acc[pos] += lax.dot_general(
            adj[g, u], err[row_ref[k]], (((0,), (0,)), ((), ())), preferred_element_type=f32
        )

    for_pairs(count, adj_hbm, adj, adj_sem, base_ref, first_ref, end_ref, work)
    grads = extra[0].astype(f32)
    for b in range(1, N_BLK):
        grads += extra[b].astype(f32)
    for i, out in enumerate(outs):
        for tile in range(XH * PER):
            at = tile * TILE
            if out.shape[0] > XH * NB and tile >= PER:
                at += EXTRA
            out[at : at + TILE] = acc[i * XH * PER + tile].astype(bf16)
        if out.shape[0] > XH * NB:
            out[NB : NB + EXTRA] = grads.astype(bf16)


def backward_tiles(scalars, adj, err):
    sizes = [XH * NB] * (2 * Z - 2) + [XH * NB + EXTRA] * 2
    nears = tuple(range(Z))
    return pl.pallas_call(
        backward_kernel,
        out_shape=[jax.ShapeDtypeStruct((size, HIDDEN), bf16) for size in sizes],
        grid_spec=pltpu.PrefetchScalarGridSpec(
            num_scalar_prefetch=4,
            grid=(),
            in_specs=[HBM, ANY],
            out_specs=[VMEM] * len(sizes),
            scratch_shapes=[
                pltpu.VMEM((TR, TILE, HIDDEN), bf16),
                pltpu.SemaphoreType.DMA((TR,)),
                pltpu.VMEM((N_BLK, EXTRA, HIDDEN), bf16),
                pltpu.SemaphoreType.DMA,
            ]
            + group_scratch(nears)
            + [pltpu.VMEM((TC + 1, TILE, HIDDEN), f32)],
        ),
        compiler_params=pltpu.CompilerParams(vmem_limit_bytes=VMEM_BYTES),
        cost_estimate=tile_cost(nears),
        name="backward_tiles",
    )(*scalars, adj, err)


def dense_kernel(scale, parts_ref, weight_ref, bias_ref, cot_ref, act_ref, back_ref):
    summed = parts_ref[0].astype(f32)
    for b in range(1, N_BLK):
        summed = summed + parts_ref[b].astype(f32)
    agg = summed.astype(bf16)
    weight = weight_ref[...]
    v = jnp.dot(agg, weight, preferred_element_type=f32) + bias_ref[...]
    c = math.sqrt(2.0 / math.pi)
    t = jnp.tanh(c * (v + 0.044715 * (v * v * v)))
    act_ref[...] = (0.5 * v * (1.0 + t)).astype(bf16)
    slope = 0.5 * (1.0 + t) + 0.5 * v * (1.0 - t * t) * (c * (1.0 + 3.0 * 0.044715 * (v * v)))
    delta = (cot_ref[...].astype(f32) * slope).astype(bf16)
    back = lax.dot_general(
        delta, weight, (((1,), (1,)), ((), ())), preferred_element_type=f32
    ).astype(bf16)
    over_nodes = (((0,), (0,)), ((), ()))
    grad_w = lax.dot_general(agg, delta, over_nodes, preferred_element_type=f32) * scale
    grad_b = jnp.sum(delta.astype(f32), axis=0, keepdims=True) * scale
    grad_b = jnp.broadcast_to(grad_b, (EXTRA - GRAD_ROWS, HIDDEN)).astype(bf16)
    for b in range(N_BLK):
        back_ref[b, :NB] = back
        back_ref[b, NB : NB + GRAD_ROWS] = grad_w[b * GRAD_ROWS : (b + 1) * GRAD_ROWS].astype(bf16)
        back_ref[b, NB + GRAD_ROWS :] = grad_b


def dense_block(parts, weight, bias, cot, scale):
    return pl.pallas_call(
        functools.partial(dense_kernel, scale),
        out_shape=[
            jax.ShapeDtypeStruct((NB, HIDDEN), bf16),
            jax.ShapeDtypeStruct((N_BLK, NB + EXTRA, HIDDEN), bf16),
        ],
        in_specs=[VMEM] * 4,
        out_specs=[VMEM] * 2,
        compiler_params=pltpu.CompilerParams(vmem_limit_bytes=VMEM_BYTES),
        name="dense_block",
    )(parts, weight, bias, cot)


def by_z_kernel(z_ref, *refs):
    total_ref, rows = refs[Z:]
    for away in range(Z):
        rows[away] = refs[away][...]
    total = jnp.zeros((EXTRA, HIDDEN), f32)
    for there in range(Z):
        total += rows[lax.rem(there - z_ref[0] + Z, Z)].astype(f32)
    total_ref[...] = total


def sum_by_z(z, parts):
    return pl.pallas_call(
        by_z_kernel,
        out_shape=jax.ShapeDtypeStruct((EXTRA, HIDDEN), f32),
        grid_spec=pltpu.PrefetchScalarGridSpec(
            num_scalar_prefetch=1,
            grid=(),
            in_specs=[VMEM] * Z,
            out_specs=VMEM,
            scratch_shapes=[pltpu.VMEM((Z, EXTRA, HIDDEN), bf16)],
        ),
        compiler_params=pltpu.CompilerParams(vmem_limit_bytes=4 * 2**20),
        name="sum_by_z",
    )(z, *parts)


def gather_forward(scalars, adj, own):
    def pair(piece):
        return [piece, swap("core")(piece)]

    both = jnp.concatenate([own, swap("xh")(own)], axis=0)
    right1, left1 = turn(both, 1), turn(both, -1)
    right2, left2 = turn(right1, 1), turn(left1, -1)
    right3, left3 = turn(right2, 1), turn(left2, -1)
    right4, left4 = turn(right3[:PER], 1), turn(left3[PER:], -1)
    near = pair(both) + pair(right1) + pair(left1) + pair(right2) + pair(left2)
    partial, zero = forward_tiles(scalars, adj, None, near, (0, 1, 2, 3, 4), False)
    ran = zero[0] == 0
    right4, left4 = jnp.where(ran, right4, left4), jnp.where(ran, left4, right4)
    far = pair(right3) + pair(left3) + [right4, left4]
    far += [swap("core")(piece) for piece in (right4, left4)]
    return forward_tiles(scalars, adj, partial, far, (5, 6, 7), True)


def place_of(cols, xh, z, core):
    owner = cols // PER
    away = ((owner // CORE) % Z - z) % Z
    near = jnp.where(away <= 3, 2 * away, 15 - 2 * away)
    return ((near * CORE + (owner % CORE ^ core)) * XH + (owner // (CORE * Z) ^ xh)) * PER + cols % PER


def backward_scatter(scalars, adj, err):
    rows = XH * NB
    outs = backward_tiles(scalars, adj, err)
    sums = [outs[2 * i].astype(f32) + swap("core")(outs[2 * i + 1]).astype(f32) for i in range(Z)]
    far = sums[7].astype(bf16)
    grads = far[NB : NB + EXTRA]
    opposite = turn(grads, Z // 2)
    right, left = turn(far[: NB + EXTRA], 1), turn(far[NB:], -1)
    from_left, from_right = [right[NB:]], [left[:EXTRA]]
    onto_right = sums[6][:NB] + right[:NB].astype(f32)
    onto_left = sums[5][NB:] + left[EXTRA:].astype(f32)
    right = jnp.concatenate(
        [onto_right.astype(bf16), sums[6][NB:].astype(bf16), from_left[0]], axis=0
    )
    left = jnp.concatenate([sums[5][:NB].astype(bf16), onto_left.astype(bf16), from_right[0]], axis=0)
    for near in (4, 2):
        right, left = turn(right, 1), turn(left, -1)
        from_left.append(right[rows:])
        from_right.append(left[rows:])
        onto_right = (sums[near] + right[:rows].astype(f32)).astype(bf16)
        onto_left = (sums[near - 1] + left[:rows].astype(f32)).astype(bf16)
        if near == 4:
            right = lax.dynamic_update_slice(right, onto_right, (0, 0))
            left = lax.dynamic_update_slice(left, onto_left, (0, 0))
    right, left = turn(onto_right, 1), turn(onto_left, -1)
    by_z = [grads] + from_right + [opposite] + from_left[::-1]
    grads = both_sides(sum_by_z(scalars[1], by_z), "xh")
    here = sums[0] + right.astype(f32) + left.astype(f32)
    across = swap("xh")(here[NB:].astype(bf16))
    return (here[:NB] + across.astype(f32)).astype(bf16), grads


def both_sides(rows, axis):
    rows = rows.astype(bf16)
    return rows.astype(f32) + swap(axis)(rows).astype(f32)


def shards(features, adj_tiles, tile_row, tile_col, weight, bias_vec, cotangent):
    adj = adj_tiles[0]
    rows = tile_row[0]
    cols = tile_col[0]
    xh, z, core = (lax.axis_index(axis) for axis in ("xh", "z", "core"))
    edges = jnp.arange(SPANS + 1, dtype=jnp.int32) * SPAN
    starts = jnp.sum((cols[None, :] < edges[:, None]).astype(jnp.int32), axis=1)
    pos = place_of(jnp.minimum(cols, TC - 1), xh, z, core)
    scalars = (starts, z.reshape(1).astype(jnp.int32), rows, pos)

    partial = gather_forward(scalars, adj, features.reshape(PER, TILE, HIDDEN))
    parts = lax.all_to_all(
        partial.reshape(N_BLK, NB, HIDDEN), BLK, split_axis=0, concat_axis=0, tiled=True
    )
    scale = 1.0 / math.sqrt(NB * XH * Z * CORE * N_BLK)
    activated, back = dense_block(parts, weight, bias_vec.reshape(1, HIDDEN), cotangent, scale)
    back = lax.all_to_all(back, BLK, split_axis=0, concat_axis=0, tiled=True)

    grad_x, grads = backward_scatter(scalars, adj, back)
    grad_w = lax.all_to_all(
        jnp.tile(grads[:GRAD_ROWS], (N_BLK, 1)), BLK, split_axis=0, concat_axis=0, tiled=True
    )
    return (activated, grad_x, grad_w, grads[GRAD_ROWS])


def solution(mesh):
    cut = Mesh(mesh.devices.reshape(XH, Z, CORE, Y, XL), AXES)
    row = ("xh", "z", "core")
    return jax.shard_map(
        shards,
        mesh=cut,
        in_specs=(
            P(AXES, None),
            P(row, BLK, None, None),
            P(row, BLK),
            P(row, BLK),
            P(),
            P(),
            P(AXES, None),
        ),
        out_specs=(P(AXES, None), P(AXES, None), P(), P()),
        check_vma=False,
    )
```

```python
import functools
import math

import jax
import jax.numpy as jnp
from jax import lax
from jax.experimental import pallas as pl
from jax.experimental.pallas import tpu as pltpu
from jax.sharding import Mesh, PartitionSpec as P

XH, Z, CORE, Y, XL = 2, 8, 2, 4, 2
AXES = ("xh", "z", "core", "y", "xl")
BLK = ("y", "xl")
N_BLK = Y * XL
TILE = 128
HIDDEN = 256
PER = 3
NB = PER * TILE
TR = N_BLK * PER
TC = XH * Z * CORE * PER
K = 288
GROUP = 16
GROUPS = K // GROUP
EXTRA = 48
GRAD_ROWS = HIDDEN // N_BLK
REST = 5 * XH * PER
VMEM_BYTES = 56 * 2**20
bf16 = jnp.bfloat16
f32 = jnp.float32

TILE_COST = pl.CostEstimate(
    flops=2 * K * TILE * TILE * HIDDEN, bytes_accessed=6 * K * TILE * TILE, transcendentals=0
)
ANY = pl.BlockSpec(memory_space=pl.ANY)
VMEM = pl.BlockSpec(memory_space=pltpu.VMEM)


def swap(axis):
    return lambda v: lax.ppermute(v, axis, [(0, 1), (1, 0)])


def turn(v, step):
    return lax.ppermute(v, "z", [(i, (i + step) % Z) for i in range(Z)])


def fetch_group(live, adj_hbm, adj, sem, g):
    first = jnp.minimum(g * GROUP, K - GROUP)
    return pltpu.make_async_copy(adj_hbm.at[pl.ds(first, GROUP)], adj.at[g], sem.at[g])


def start_groups(live_ref, adj_hbm, adj, sem):
    live = live_ref[0]
    groups = (live + GROUP - 1) // GROUP

    def begin(g, carry):
        fetch_group(live, adj_hbm, adj, sem, g).start()
        return carry

    lax.fori_loop(0, groups, begin, 0)
    return live, groups


def forward_kernel(live_ref, row_ref, pos_ref, adj_hbm, *refs):
    pieces = refs[:-6]
    out_ref, adj, slab, acc, adj_sem, piece_sem = refs[-6:]
    copies = []
    at = 0
    for n, piece in enumerate(pieces):
        size = piece.shape[0]
        copies.append(pltpu.make_async_copy(piece, slab.at[pl.ds(at, size)], piece_sem.at[n]))
        at += size
    for copy in copies:
        copy.start()
    live, groups = start_groups(live_ref, adj_hbm, adj, adj_sem)
    acc[...] = jnp.zeros_like(acc)
    for copy in copies:
        copy.wait()

    def step(g, carry):
        fetch_group(live, adj_hbm, adj, adj_sem, g).wait()
        for u in range(GROUP):
            k = g * GROUP + u
            row = jnp.where(k < live, row_ref[k], TR)
            acc[row] += jnp.dot(adj[g, u], slab[pos_ref[k]], preferred_element_type=f32)
        return carry

    lax.fori_loop(0, groups, step, 0)
    out_ref[...] = acc[:TR].astype(bf16)


def forward_tiles(live, rows, pos, adj, pieces):
    return pl.pallas_call(
        forward_kernel,
        out_shape=jax.ShapeDtypeStruct((TR, TILE, HIDDEN), bf16),
        grid_spec=pltpu.PrefetchScalarGridSpec(
            num_scalar_prefetch=3,
            grid=(),
            in_specs=[ANY] * (1 + len(pieces)),
            out_specs=VMEM,
            scratch_shapes=[
                pltpu.VMEM((GROUPS, GROUP, TILE, TILE), bf16),
                pltpu.VMEM((TC, TILE, HIDDEN), bf16),
                pltpu.VMEM((TR + 1, TILE, HIDDEN), f32),
                pltpu.SemaphoreType.DMA((GROUPS,)),
                pltpu.SemaphoreType.DMA((len(pieces),)),
            ],
        ),
        compiler_params=pltpu.CompilerParams(vmem_limit_bytes=VMEM_BYTES),
        cost_estimate=TILE_COST,
        name="forward_tiles",
    )(live, rows, pos, adj, *pieces)


def backward_kernel(live_ref, row_ref, pos_ref, adj_hbm, err_hbm, *refs):
    outs = refs[:-5]
    adj, err, acc, adj_sem, err_sem = refs[-5:]
    copies = [
        pltpu.make_async_copy(
            err_hbm.at[i // PER, pl.ds(i % PER * TILE, TILE)], err.at[i], err_sem.at[i]
        )
        for i in range(TR)
    ]
    for copy in copies:
        copy.start()
    live, groups = start_groups(live_ref, adj_hbm, adj, adj_sem)
    acc[...] = jnp.zeros_like(acc)
    for copy in copies:
        copy.wait()

    def step(g, carry):
        fetch_group(live, adj_hbm, adj, adj_sem, g).wait()
        for u in range(GROUP):
            k = g * GROUP + u
            pos = jnp.where(k < live, pos_ref[k], TC)
            acc[pos] += lax.dot_general(
                adj[g, u], err[row_ref[k]], (((0,), (0,)), ((), ())), preferred_element_type=f32
            )
        return carry

    lax.fori_loop(0, groups, step, 0)
    half = TC // CORE
    for core in range(CORE):
        far, rest = outs[2 * core : 2 * core + 2]
        rest[...] = acc[core * half : core * half + REST].astype(bf16)
        far[...] = acc[core * half + REST : (core + 1) * half].astype(bf16)


def backward_tiles(live, rows, pos, adj, err):
    return pl.pallas_call(
        backward_kernel,
        out_shape=[
            jax.ShapeDtypeStruct((tiles, TILE, HIDDEN), bf16) for tiles in (TC // CORE - REST, REST)
        ]
        * CORE,
        grid_spec=pltpu.PrefetchScalarGridSpec(
            num_scalar_prefetch=3,
            grid=(),
            in_specs=[ANY, ANY],
            out_specs=[VMEM] * (2 * CORE),
            scratch_shapes=[
                pltpu.VMEM((GROUPS, GROUP, TILE, TILE), bf16),
                pltpu.VMEM((TR, TILE, HIDDEN), bf16),
                pltpu.VMEM((TC + 1, TILE, HIDDEN), f32),
                pltpu.SemaphoreType.DMA((GROUPS,)),
                pltpu.SemaphoreType.DMA((TR,)),
            ],
        ),
        compiler_params=pltpu.CompilerParams(vmem_limit_bytes=VMEM_BYTES),
        cost_estimate=TILE_COST,
        name="backward_tiles",
    )(live, rows, pos, adj, err)


def dense_kernel(scale, parts_ref, weight_ref, bias_ref, cot_ref, act_ref, back_ref):
    summed = parts_ref[0].astype(f32)
    for b in range(1, N_BLK):
        summed = summed + parts_ref[b].astype(f32)
    agg = summed.astype(bf16)
    weight = weight_ref[...]
    v = jnp.dot(agg, weight, preferred_element_type=f32) + bias_ref[...]
    c = math.sqrt(2.0 / math.pi)
    t = jnp.tanh(c * (v + 0.044715 * (v * v * v)))
    act_ref[...] = (0.5 * v * (1.0 + t)).astype(bf16)
    slope = 0.5 * (1.0 + t) + 0.5 * v * (1.0 - t * t) * (c * (1.0 + 3.0 * 0.044715 * (v * v)))
    delta = (cot_ref[...].astype(f32) * slope).astype(bf16)
    back = lax.dot_general(
        delta, weight, (((1,), (1,)), ((), ())), preferred_element_type=f32
    ).astype(bf16)
    over_nodes = (((0,), (0,)), ((), ()))
    grad_w = lax.dot_general(agg, delta, over_nodes, preferred_element_type=f32) * scale
    grad_b = jnp.sum(delta.astype(f32), axis=0, keepdims=True) * scale
    grad_b = jnp.broadcast_to(grad_b, (EXTRA - GRAD_ROWS, HIDDEN)).astype(bf16)
    for b in range(N_BLK):
        back_ref[b, :NB] = back
        back_ref[b, NB : NB + GRAD_ROWS] = grad_w[b * GRAD_ROWS : (b + 1) * GRAD_ROWS].astype(bf16)
        back_ref[b, NB + GRAD_ROWS :] = grad_b


def dense_block(parts, weight, bias, cot, scale):
    return pl.pallas_call(
        functools.partial(dense_kernel, scale),
        out_shape=[
            jax.ShapeDtypeStruct((NB, HIDDEN), bf16),
            jax.ShapeDtypeStruct((N_BLK, NB + EXTRA, HIDDEN), bf16),
        ],
        in_specs=[VMEM] * 4,
        out_specs=[VMEM] * 2,
        compiler_params=pltpu.CompilerParams(vmem_limit_bytes=VMEM_BYTES),
        name="dense_block",
    )(parts, weight, bias, cot)


def gather_pieces(own):
    here, across = own, swap("xh")(own)
    near = [(here, across)]
    right = left = near[0]
    for _ in range(3):
        right = tuple(turn(v, 1) for v in right)
        left = tuple(turn(v, -1) for v in left)
        near += [right, left]
    near.append((turn(right[0], 1), turn(left[1], -1)))
    pieces = []
    for pair in near:
        pieces += [*pair, *(swap("core")(v) for v in pair)]
    return pieces


def place_of(cols, xh, z, core):
    owner = cols // PER
    away = ((owner // CORE) % Z - z) % Z
    near = jnp.where(away <= 3, 2 * away, 15 - 2 * away)
    return near, (owner % CORE) ^ core, (owner // (CORE * Z)) ^ xh, cols % PER


def scatter_sum(keep, sends):
    received = [swap("core")(part) for part in sends]

    def mine(near, xh, size=PER):
        at = (near * XH + xh) * PER
        part = 0 if at >= REST else 1
        at = at - REST if at >= REST else at
        return keep[part][at : at + size].astype(f32) + received[part][at : at + size].astype(f32)

    def send(near, xh, carried, step):
        total = mine(near, xh)
        if carried is not None:
            total = total + carried.astype(f32)
        return turn(total.astype(bf16), step)

    far = mine(7, 0, XH * PER).astype(bf16)
    right, left = [turn(far[:PER], 1), None], [None, turn(far[PER:], -1)]
    for near in (6, 4, 2):
        for xh in (1, 0):
            right[xh] = send(near, xh, right[xh], 1)
            left[xh] = send(near - 1, xh, left[xh], -1)
        if near == 6:
            second = right[0]
    here, across = (mine(0, xh) + right[xh].astype(f32) + left[xh].astype(f32) for xh in (0, 1))
    across = swap("xh")(across.astype(bf16))
    return (here + across.astype(f32)).astype(bf16), second, right[1]


def both_sides(rows, axis):
    rows = rows.astype(bf16)
    return rows.astype(f32) + swap(axis)(rows).astype(f32)


def shards(features, adj_tiles, tile_row, tile_col, weight, bias_vec, cotangent):
    adj = adj_tiles[0]
    rows = tile_row[0]
    cols = tile_col[0]
    xh, z, core = (lax.axis_index(axis) for axis in ("xh", "z", "core"))
    live = jnp.sum((cols < TC).astype(jnp.int32)).reshape(1)
    near, other, across, part = place_of(jnp.minimum(cols, TC - 1), xh, z, core)
    slab_pos = ((near * CORE + other) * XH + across) * PER + part
    sum_pos = ((other * Z + near) * XH + across) * PER + part

    pieces = gather_pieces(features.reshape(PER, TILE, HIDDEN))
    partial = forward_tiles(live, rows, slab_pos, adj, pieces)
    parts = lax.all_to_all(
        partial.reshape(N_BLK, NB, HIDDEN), BLK, split_axis=0, concat_axis=0, tiled=True
    )
    scale = 1.0 / math.sqrt(NB * XH * Z * CORE * N_BLK)
    activated, back = dense_block(parts, weight, bias_vec.reshape(1, HIDDEN), cotangent, scale)
    back = lax.all_to_all(back, BLK, split_axis=0, concat_axis=0, tiled=True)

    outs = backward_tiles(live, rows, sum_pos, adj, back)
    grad_x, second, last = scatter_sum(outs[:2], outs[2:])

    grads = jnp.sum(back[:, NB:].astype(f32), axis=0)
    grads = both_sides(both_sides(grads, "core"), "xh")
    grads = (grads + 0.0 * second[0, :EXTRA].astype(f32)).astype(bf16)
    by_z = lax.all_to_all(jnp.tile(grads, (Z, 1)), "z", split_axis=0, concat_axis=0, tiled=True)
    grads = jnp.sum(by_z.reshape(Z, EXTRA, HIDDEN).astype(f32), axis=0)
    grads = grads + 0.0 * last[0, :EXTRA].astype(f32)
    grad_w = lax.all_to_all(
        jnp.tile(grads[:GRAD_ROWS], (N_BLK, 1)), BLK, split_axis=0, concat_axis=0, tiled=True
    )
    return (activated, grad_x.reshape(NB, HIDDEN), grad_w, grads[GRAD_ROWS])


def solution(mesh):
    cut = Mesh(mesh.devices.reshape(XH, Z, CORE, Y, XL), AXES)
    row = ("xh", "z", "core")
    return jax.shard_map(
        shards,
        mesh=cut,
        in_specs=(
            P(AXES, None),
            P(row, BLK, None, None),
            P(row, BLK),
            P(row, BLK),
            P(),
            P(),
            P(AXES, None),
        ),
        out_specs=(P(AXES, None), P(AXES, None), P(), P()),
        check_vma=False,
    )
```

```python
import functools
import math

import jax
import jax.numpy as jnp
from jax import lax
from jax.experimental import pallas as pl
from jax.experimental.pallas import tpu as pltpu
from jax.sharding import Mesh, PartitionSpec as P

XH, Z, CORE, Y, XL = 2, 8, 2, 4, 2
AXES = ("xh", "z", "core", "y", "xl")
BLK = ("y", "xl")
N_BLK = Y * XL
TILE = 128
HIDDEN = 256
PER = 3
NB = PER * TILE
TR = N_BLK * PER
TC = XH * Z * CORE * PER
K = 288
GROUP = 16
GROUPS = K // GROUP
EXTRA = 48
GRAD_ROWS = HIDDEN // N_BLK
CHAIN = Z // 2 * PER
VMEM_BYTES = 56 * 2**20
bf16 = jnp.bfloat16
f32 = jnp.float32

TILE_COST = pl.CostEstimate(
    flops=2 * K * TILE * TILE * HIDDEN, bytes_accessed=6 * K * TILE * TILE, transcendentals=0
)
ANY = pl.BlockSpec(memory_space=pl.ANY)
VMEM = pl.BlockSpec(memory_space=pltpu.VMEM)


def swap(axis):
    return lambda v: lax.ppermute(v, axis, [(0, 1), (1, 0)])


def turn(v, step):
    return lax.ppermute(v, "z", [(i, (i + step) % Z) for i in range(Z)])


def fetch_group(live, adj_hbm, adj, sem, g):
    first = jnp.minimum(g * GROUP, K - GROUP)
    return pltpu.make_async_copy(adj_hbm.at[pl.ds(first, GROUP)], adj.at[g], sem.at[g])


def start_groups(live_ref, adj_hbm, adj, sem):
    live = live_ref[0]
    groups = (live + GROUP - 1) // GROUP

    def begin(g, carry):
        fetch_group(live, adj_hbm, adj, sem, g).start()
        return carry

    lax.fori_loop(0, groups, begin, 0)
    return live, groups


def forward_kernel(live_ref, row_ref, pos_ref, adj_hbm, *refs):
    pieces = refs[:-6]
    out_ref, adj, slab, acc, adj_sem, piece_sem = refs[-6:]
    copies = []
    at = 0
    for n, piece in enumerate(pieces):
        size = piece.shape[0]
        copies.append(pltpu.make_async_copy(piece, slab.at[pl.ds(at, size)], piece_sem.at[n]))
        at += size
    for copy in copies:
        copy.start()
    live, groups = start_groups(live_ref, adj_hbm, adj, adj_sem)
    acc[...] = jnp.zeros_like(acc)
    for copy in copies:
        copy.wait()

    def step(g, carry):
        fetch_group(live, adj_hbm, adj, adj_sem, g).wait()
        for u in range(GROUP):
            k = g * GROUP + u
            row = jnp.where(k < live, row_ref[k], TR)
            acc[row] += jnp.dot(adj[g, u], slab[pos_ref[k]], preferred_element_type=f32)
        return carry

    lax.fori_loop(0, groups, step, 0)
    out_ref[...] = acc[:TR].astype(bf16)


def forward_tiles(live, rows, pos, adj, pieces):
    return pl.pallas_call(
        forward_kernel,
        out_shape=jax.ShapeDtypeStruct((TR, TILE, HIDDEN), bf16),
        grid_spec=pltpu.PrefetchScalarGridSpec(
            num_scalar_prefetch=3,
            grid=(),
            in_specs=[ANY] * (1 + len(pieces)),
            out_specs=VMEM,
            scratch_shapes=[
                pltpu.VMEM((GROUPS, GROUP, TILE, TILE), bf16),
                pltpu.VMEM((TC, TILE, HIDDEN), bf16),
                pltpu.VMEM((TR + 1, TILE, HIDDEN), f32),
                pltpu.SemaphoreType.DMA((GROUPS,)),
                pltpu.SemaphoreType.DMA((len(pieces),)),
            ],
        ),
        compiler_params=pltpu.CompilerParams(vmem_limit_bytes=VMEM_BYTES),
        cost_estimate=TILE_COST,
        name="forward_tiles",
    )(live, rows, pos, adj, *pieces)


def backward_kernel(live_ref, row_ref, pos_ref, adj_hbm, err_hbm, *refs):
    outs = refs[:-5]
    adj, err, acc, adj_sem, err_sem = refs[-5:]
    copies = [
        pltpu.make_async_copy(
            err_hbm.at[i // PER, pl.ds(i % PER * TILE, TILE)], err.at[i], err_sem.at[i]
        )
        for i in range(TR)
    ]
    for copy in copies:
        copy.start()
    live, groups = start_groups(live_ref, adj_hbm, adj, adj_sem)
    acc[...] = jnp.zeros_like(acc)
    for copy in copies:
        copy.wait()

    def step(g, carry):
        fetch_group(live, adj_hbm, adj, adj_sem, g).wait()
        for u in range(GROUP):
            k = g * GROUP + u
            pos = jnp.where(k < live, pos_ref[k], TC)
            acc[pos] += lax.dot_general(
                adj[g, u], err[row_ref[k]], (((0,), (0,)), ((), ())), preferred_element_type=f32
            )
        return carry

    lax.fori_loop(0, groups, step, 0)
    for i, out in enumerate(outs):
        out[...] = acc[i * CHAIN : (i + 1) * CHAIN].astype(bf16)


def backward_tiles(live, rows, pos, adj, err):
    return pl.pallas_call(
        backward_kernel,
        out_shape=[jax.ShapeDtypeStruct((CHAIN, TILE, HIDDEN), bf16)] * (TC // CHAIN),
        grid_spec=pltpu.PrefetchScalarGridSpec(
            num_scalar_prefetch=3,
            grid=(),
            in_specs=[ANY, ANY],
            out_specs=[VMEM] * (TC // CHAIN),
            scratch_shapes=[
                pltpu.VMEM((GROUPS, GROUP, TILE, TILE), bf16),
                pltpu.VMEM((TR, TILE, HIDDEN), bf16),
                pltpu.VMEM((TC + 1, TILE, HIDDEN), f32),
                pltpu.SemaphoreType.DMA((GROUPS,)),
                pltpu.SemaphoreType.DMA((TR,)),
            ],
        ),
        compiler_params=pltpu.CompilerParams(vmem_limit_bytes=VMEM_BYTES),
        cost_estimate=TILE_COST,
        name="backward_tiles",
    )(live, rows, pos, adj, err)


def dense_kernel(scale, parts_ref, weight_ref, bias_ref, cot_ref, act_ref, back_ref):
    summed = parts_ref[0].astype(f32)
    for b in range(1, N_BLK):
        summed = summed + parts_ref[b].astype(f32)
    agg = summed.astype(bf16)
    weight = weight_ref[...]
    v = jnp.dot(agg, weight, preferred_element_type=f32) + bias_ref[...]
    c = math.sqrt(2.0 / math.pi)
    t = jnp.tanh(c * (v + 0.044715 * (v * v * v)))
    act_ref[...] = (0.5 * v * (1.0 + t)).astype(bf16)
    slope = 0.5 * (1.0 + t) + 0.5 * v * (1.0 - t * t) * (c * (1.0 + 3.0 * 0.044715 * (v * v)))
    delta = (cot_ref[...].astype(f32) * slope).astype(bf16)
    back = lax.dot_general(
        delta, weight, (((1,), (1,)), ((), ())), preferred_element_type=f32
    ).astype(bf16)
    over_nodes = (((0,), (0,)), ((), ()))
    grad_w = lax.dot_general(agg, delta, over_nodes, preferred_element_type=f32) * scale
    grad_b = jnp.sum(delta.astype(f32), axis=0, keepdims=True) * scale
    grad_b = jnp.broadcast_to(grad_b, (EXTRA - GRAD_ROWS, HIDDEN)).astype(bf16)
    for b in range(N_BLK):
        back_ref[b, :NB] = back
        back_ref[b, NB : NB + GRAD_ROWS] = grad_w[b * GRAD_ROWS : (b + 1) * GRAD_ROWS].astype(bf16)
        back_ref[b, NB + GRAD_ROWS :] = grad_b


def dense_block(parts, weight, bias, cot, scale):
    return pl.pallas_call(
        functools.partial(dense_kernel, scale),
        out_shape=[
            jax.ShapeDtypeStruct((NB, HIDDEN), bf16),
            jax.ShapeDtypeStruct((N_BLK, NB + EXTRA, HIDDEN), bf16),
        ],
        in_specs=[VMEM] * 4,
        out_specs=[VMEM] * 2,
        compiler_params=pltpu.CompilerParams(vmem_limit_bytes=VMEM_BYTES),
        name="dense_block",
    )(parts, weight, bias, cot)


def gather_pieces(own):
    across = swap("xh")
    right, left = [own], [own]
    right_across = [across(own)]
    left_across = list(right_across)
    for step in range(1, 4):
        right.append(turn(right[-1], 1))
        left.append(turn(left[-1], -1))
        right_across.append(turn(right_across[-1], 1) if step < 2 else across(right[-1]))
        left_across.append(turn(left_across[-1], -1) if step < 3 else across(left[-1]))
    near = [(own, right_across[0])]
    for step in range(1, 4):
        near += [(right[step], right_across[step]), (left[step], left_across[step])]
    last = turn(right[3], 1)
    near.append((last, across(last)))
    pieces = []
    for pair in near:
        pieces += [*pair, *(swap("core")(v) for v in pair)]
    return pieces


def place_of(cols, xh, z, core):
    owner = cols // PER
    away = ((owner // CORE) % Z - z) % Z
    near = jnp.where(away <= 3, 2 * away, 15 - 2 * away)
    return near, (owner % CORE) ^ core, (owner // (CORE * Z)) ^ xh, cols % PER


def scatter_sum(keep, sends):
    received = [None] * 4
    for chain in (3, 1, 2, 0):
        received[chain] = swap("core")(sends[chain])

    def mine(near, xh):
        chain, at = xh * 2 + near % 2, near // 2 * PER
        return keep[chain][at : at + PER].astype(f32) + received[chain][at : at + PER].astype(f32)

    def pass_on(total, step):
        return turn(total.astype(bf16), step).astype(f32)

    crossed = [swap("xh")(mine(near, 1).astype(bf16)).astype(f32) for near in (7, 5, 6)]
    right_across = pass_on(mine(4, 1), 1)
    left_across = pass_on(mine(3, 1), -1)
    early = right_across[0, :EXTRA] + left_across[0, :EXTRA]
    left = pass_on(mine(7, 0) + crossed[0], -1)
    right = pass_on(mine(6, 0) + crossed[2], 1)
    right_across = pass_on(mine(2, 1) + right_across, 1)
    left_across = pass_on(mine(1, 1) + left_across, -1)
    left = pass_on(mine(5, 0) + crossed[1] + left, -1)
    right = pass_on(mine(4, 0) + right, 1)
    across = mine(0, 1) + right_across + left_across
    across = swap("xh")(across.astype(bf16))
    left = pass_on(mine(3, 0) + left, -1)
    late = left[0, :EXTRA]
    right = pass_on(mine(2, 0) + right, 1)
    left = pass_on(mine(1, 0) + left, -1)
    here = mine(0, 0) + right + left
    return (here + across.astype(f32)).astype(bf16), early, late


def both_sides(rows, axis):
    rows = rows.astype(bf16)
    return rows.astype(f32) + swap(axis)(rows).astype(f32)


def shards(features, adj_tiles, tile_row, tile_col, weight, bias_vec, cotangent):
    adj = adj_tiles[0]
    rows = tile_row[0]
    cols = tile_col[0]
    xh, z, core = (lax.axis_index(axis) for axis in ("xh", "z", "core"))
    live = jnp.sum((cols < TC).astype(jnp.int32)).reshape(1)
    near, other, across, part = place_of(jnp.minimum(cols, TC - 1), xh, z, core)
    slab_pos = ((near * CORE + other) * XH + across) * PER + part
    sum_pos = (((other * XH + across) * 2 + near % 2) * (Z // 2) + near // 2) * PER + part

    pieces = gather_pieces(features.reshape(PER, TILE, HIDDEN))
    partial = forward_tiles(live, rows, slab_pos, adj, pieces)
    parts = lax.all_to_all(
        partial.reshape(N_BLK, NB, HIDDEN), BLK, split_axis=0, concat_axis=0, tiled=True
    )
    scale = 1.0 / math.sqrt(NB * XH * Z * CORE * N_BLK)
    activated, back = dense_block(parts, weight, bias_vec.reshape(1, HIDDEN), cotangent, scale)
    back = lax.all_to_all(back, BLK, split_axis=0, concat_axis=0, tiled=True)

    outs = backward_tiles(live, rows, sum_pos, adj, back)
    grad_x, early, late = scatter_sum(outs[:4], outs[4:])

    grads = jnp.sum(back[:, NB:].astype(f32), axis=0)
    grads = both_sides(both_sides(grads, "core"), "xh")
    grads = (grads + 0.0 * early).astype(bf16)
    by_z = lax.all_to_all(jnp.tile(grads, (Z, 1)), "z", split_axis=0, concat_axis=0, tiled=True)
    grads = jnp.sum(by_z.reshape(Z, EXTRA, HIDDEN).astype(f32), axis=0)
    grads = grads + 0.0 * late
    grad_w = lax.all_to_all(
        jnp.tile(grads[:GRAD_ROWS], (N_BLK, 1)), BLK, split_axis=0, concat_axis=0, tiled=True
    )
    return (activated, grad_x.reshape(NB, HIDDEN), grad_w, grads[GRAD_ROWS])


def solution(mesh):
    cut = Mesh(mesh.devices.reshape(XH, Z, CORE, Y, XL), AXES)
    row = ("xh", "z", "core")
    return jax.shard_map(
        shards,
        mesh=cut,
        in_specs=(
            P(AXES, None),
            P(row, BLK, None, None),
            P(row, BLK),
            P(row, BLK),
            P(),
            P(),
            P(AXES, None),
        ),
        out_specs=(P(AXES, None), P(AXES, None), P(), P()),
        check_vma=False,
    )
```

```python
import functools
import math

import jax
import jax.numpy as jnp
from jax import lax
from jax.experimental import pallas as pl
from jax.experimental.pallas import tpu as pltpu
from jax.sharding import Mesh, PartitionSpec as P

XH, Z, CORE, Y, XL = 2, 8, 2, 4, 2
AXES = ("xh", "z", "core", "y", "xl")
BLK = ("y", "xl")
N_BLK = Y * XL
TILE = 128
HIDDEN = 256
PER = 3
NB = PER * TILE
TR = N_BLK * PER
TC = XH * Z * CORE * PER
K = 288
GROUP = 16
GROUPS = K // GROUP
EXTRA = 48
GRAD_ROWS = HIDDEN // N_BLK
CHAIN = Z // 2 * XH * PER
VMEM_BYTES = 56 * 2**20
bf16 = jnp.bfloat16
f32 = jnp.float32

TILE_COST = pl.CostEstimate(
    flops=2 * K * TILE * TILE * HIDDEN, bytes_accessed=6 * K * TILE * TILE, transcendentals=0
)
ANY = pl.BlockSpec(memory_space=pl.ANY)
VMEM = pl.BlockSpec(memory_space=pltpu.VMEM)


def swap(axis):
    return lambda v: lax.ppermute(v, axis, [(0, 1), (1, 0)])


def turn(v, step):
    return lax.ppermute(v, "z", [(i, (i + step) % Z) for i in range(Z)])


def fetch_group(live, adj_hbm, adj, sem, g):
    first = jnp.minimum(g * GROUP, K - GROUP)
    return pltpu.make_async_copy(adj_hbm.at[pl.ds(first, GROUP)], adj.at[g], sem.at[g])


def start_groups(live_ref, adj_hbm, adj, sem):
    live = live_ref[0]
    groups = (live + GROUP - 1) // GROUP

    def begin(g, carry):
        fetch_group(live, adj_hbm, adj, sem, g).start()
        return carry

    lax.fori_loop(0, groups, begin, 0)
    return live, groups


def forward_kernel(live_ref, row_ref, pos_ref, adj_hbm, *refs):
    pieces = refs[:-6]
    out_ref, adj, slab, acc, adj_sem, piece_sem = refs[-6:]
    copies = []
    at = 0
    for n, piece in enumerate(pieces):
        size = piece.shape[0]
        copies.append(pltpu.make_async_copy(piece, slab.at[pl.ds(at, size)], piece_sem.at[n]))
        at += size
    for copy in copies:
        copy.start()
    live, groups = start_groups(live_ref, adj_hbm, adj, adj_sem)
    acc[...] = jnp.zeros_like(acc)
    for copy in copies:
        copy.wait()

    def step(g, carry):
        fetch_group(live, adj_hbm, adj, adj_sem, g).wait()
        for u in range(GROUP):
            k = g * GROUP + u
            row = jnp.where(k < live, row_ref[k], TR)
            acc[row] += jnp.dot(adj[g, u], slab[pos_ref[k]], preferred_element_type=f32)
        return carry

    lax.fori_loop(0, groups, step, 0)
    out_ref[...] = acc[:TR].astype(bf16)


def forward_tiles(live, rows, pos, adj, pieces):
    return pl.pallas_call(
        forward_kernel,
        out_shape=jax.ShapeDtypeStruct((TR, TILE, HIDDEN), bf16),
        grid_spec=pltpu.PrefetchScalarGridSpec(
            num_scalar_prefetch=3,
            grid=(),
            in_specs=[ANY] * (1 + len(pieces)),
            out_specs=VMEM,
            scratch_shapes=[
                pltpu.VMEM((GROUPS, GROUP, TILE, TILE), bf16),
                pltpu.VMEM((TC, TILE, HIDDEN), bf16),
                pltpu.VMEM((TR + 1, TILE, HIDDEN), f32),
                pltpu.SemaphoreType.DMA((GROUPS,)),
                pltpu.SemaphoreType.DMA((len(pieces),)),
            ],
        ),
        compiler_params=pltpu.CompilerParams(vmem_limit_bytes=VMEM_BYTES),
        cost_estimate=TILE_COST,
        name="forward_tiles",
    )(live, rows, pos, adj, *pieces)


def backward_kernel(live_ref, row_ref, pos_ref, adj_hbm, err_hbm, *refs):
    outs = refs[:-5]
    adj, err, acc, adj_sem, err_sem = refs[-5:]
    copies = [
        pltpu.make_async_copy(
            err_hbm.at[i // PER, pl.ds(i % PER * TILE, TILE)], err.at[i], err_sem.at[i]
        )
        for i in range(TR)
    ]
    for copy in copies:
        copy.start()
    live, groups = start_groups(live_ref, adj_hbm, adj, adj_sem)
    acc[...] = jnp.zeros_like(acc)
    for copy in copies:
        copy.wait()

    def step(g, carry):
        fetch_group(live, adj_hbm, adj, adj_sem, g).wait()
        for u in range(GROUP):
            k = g * GROUP + u
            pos = jnp.where(k < live, pos_ref[k], TC)
            acc[pos] += lax.dot_general(
                adj[g, u], err[row_ref[k]], (((0,), (0,)), ((), ())), preferred_element_type=f32
            )
        return carry

    lax.fori_loop(0, groups, step, 0)
    for i, out in enumerate(outs):
        out[...] = acc[i * CHAIN : (i + 1) * CHAIN].astype(bf16)


def backward_tiles(live, rows, pos, adj, err):
    return pl.pallas_call(
        backward_kernel,
        out_shape=[jax.ShapeDtypeStruct((CHAIN, TILE, HIDDEN), bf16)] * (TC // CHAIN),
        grid_spec=pltpu.PrefetchScalarGridSpec(
            num_scalar_prefetch=3,
            grid=(),
            in_specs=[ANY, ANY],
            out_specs=[VMEM] * (TC // CHAIN),
            scratch_shapes=[
                pltpu.VMEM((GROUPS, GROUP, TILE, TILE), bf16),
                pltpu.VMEM((TR, TILE, HIDDEN), bf16),
                pltpu.VMEM((TC + 1, TILE, HIDDEN), f32),
                pltpu.SemaphoreType.DMA((GROUPS,)),
                pltpu.SemaphoreType.DMA((TR,)),
            ],
        ),
        compiler_params=pltpu.CompilerParams(vmem_limit_bytes=VMEM_BYTES),
        cost_estimate=TILE_COST,
        name="backward_tiles",
    )(live, rows, pos, adj, err)


def dense_kernel(scale, parts_ref, weight_ref, bias_ref, cot_ref, act_ref, back_ref):
    summed = parts_ref[0].astype(f32)
    for b in range(1, N_BLK):
        summed = summed + parts_ref[b].astype(f32)
    agg = summed.astype(bf16)
    weight = weight_ref[...]
    v = jnp.dot(agg, weight, preferred_element_type=f32) + bias_ref[...]
    c = math.sqrt(2.0 / math.pi)
    t = jnp.tanh(c * (v + 0.044715 * (v * v * v)))
    act_ref[...] = (0.5 * v * (1.0 + t)).astype(bf16)
    slope = 0.5 * (1.0 + t) + 0.5 * v * (1.0 - t * t) * (c * (1.0 + 3.0 * 0.044715 * (v * v)))
    delta = (cot_ref[...].astype(f32) * slope).astype(bf16)
    back = lax.dot_general(
        delta, weight, (((1,), (1,)), ((), ())), preferred_element_type=f32
    ).astype(bf16)
    over_nodes = (((0,), (0,)), ((), ()))
    grad_w = lax.dot_general(agg, delta, over_nodes, preferred_element_type=f32) * scale
    grad_b = jnp.sum(delta.astype(f32), axis=0, keepdims=True) * scale
    grad_b = jnp.broadcast_to(grad_b, (EXTRA - GRAD_ROWS, HIDDEN)).astype(bf16)
    for b in range(N_BLK):
        back_ref[b, :NB] = back
        back_ref[b, NB : NB + GRAD_ROWS] = grad_w[b * GRAD_ROWS : (b + 1) * GRAD_ROWS].astype(bf16)
        back_ref[b, NB + GRAD_ROWS :] = grad_b


def dense_block(parts, weight, bias, cot, scale):
    return pl.pallas_call(
        functools.partial(dense_kernel, scale),
        out_shape=[
            jax.ShapeDtypeStruct((NB, HIDDEN), bf16),
            jax.ShapeDtypeStruct((N_BLK, NB + EXTRA, HIDDEN), bf16),
        ],
        in_specs=[VMEM] * 4,
        out_specs=[VMEM] * 2,
        compiler_params=pltpu.CompilerParams(vmem_limit_bytes=VMEM_BYTES),
        name="dense_block",
    )(parts, weight, bias, cot)


def gather_pieces(own):
    here, across = own, swap("xh")(own)
    near = [(here, across)]
    right = left = near[0]
    for _ in range(3):
        right = tuple(turn(v, 1) for v in right)
        left = tuple(turn(v, -1) for v in left)
        near += [right, left]
    near.append((turn(right[0], 1), turn(left[1], -1)))
    pieces = []
    for pair in near:
        pieces += [*pair, *(swap("core")(v) for v in pair)]
    return pieces


def place_of(cols, xh, z, core):
    owner = cols // PER
    away = ((owner // CORE) % Z - z) % Z
    near = jnp.where(away <= 3, 2 * away, 15 - 2 * away)
    return near, (owner % CORE) ^ core, (owner // (CORE * Z)) ^ xh, cols % PER


def scatter_sum(keep, sends):
    odd = swap("core")(sends[1])
    received = [swap("core")(sends[0]), odd]

    def mine(near):
        at = slice(near // 2 * XH * PER, (near // 2 + 1) * XH * PER)
        return keep[near % 2][at].astype(f32) + received[near % 2][at].astype(f32)

    far = mine(7).astype(bf16)
    right, left = turn(far[:PER], 1), turn(far[PER:], -1)
    first = right[0, :EXTRA].astype(f32) + left[0, :EXTRA].astype(f32)
    onto_right, onto_left = mine(6), mine(5)
    right = jnp.concatenate([onto_right[:PER] + right.astype(f32), onto_right[PER:]], axis=0)
    left = jnp.concatenate([onto_left[:PER], onto_left[PER:] + left.astype(f32)], axis=0)
    for near in (4, 2):
        right, left = turn(right.astype(bf16), 1), turn(left.astype(bf16), -1)
        third = right[0, :EXTRA].astype(f32) + left[0, :EXTRA].astype(f32)
        right = mine(near) + right.astype(f32)
        left = mine(near - 1) + left.astype(f32)
    here = mine(0) + turn(right.astype(bf16), 1).astype(f32) + turn(left.astype(bf16), -1).astype(f32)
    across = swap("xh")(here[PER:].astype(bf16))
    return (here[:PER] + across.astype(f32)).astype(bf16), first, third


def both_sides(rows, axis):
    rows = rows.astype(bf16)
    return rows.astype(f32) + swap(axis)(rows).astype(f32)


def shards(features, adj_tiles, tile_row, tile_col, weight, bias_vec, cotangent):
    adj = adj_tiles[0]
    rows = tile_row[0]
    cols = tile_col[0]
    xh, z, core = (lax.axis_index(axis) for axis in ("xh", "z", "core"))
    live = jnp.sum((cols < TC).astype(jnp.int32)).reshape(1)
    near, other, across, part = place_of(jnp.minimum(cols, TC - 1), xh, z, core)
    slab_pos = ((near * CORE + other) * XH + across) * PER + part
    sum_pos = (((other * 2 + near % 2) * (Z // 2) + near // 2) * XH + across) * PER + part

    pieces = gather_pieces(features.reshape(PER, TILE, HIDDEN))
    partial = forward_tiles(live, rows, slab_pos, adj, pieces)
    parts = lax.all_to_all(
        partial.reshape(N_BLK, NB, HIDDEN), BLK, split_axis=0, concat_axis=0, tiled=True
    )
    scale = 1.0 / math.sqrt(NB * XH * Z * CORE * N_BLK)
    activated, back = dense_block(parts, weight, bias_vec.reshape(1, HIDDEN), cotangent, scale)
    back = lax.all_to_all(back, BLK, split_axis=0, concat_axis=0, tiled=True)

    outs = backward_tiles(live, rows, sum_pos, adj, back)
    grad_x, first, third = scatter_sum(outs[:2], outs[2:])

    grads = jnp.sum(back[:, NB:].astype(f32), axis=0)
    grads = both_sides(both_sides(grads, "core"), "xh")
    grads = (grads + 0.0 * first).astype(bf16)
    by_z = lax.all_to_all(jnp.tile(grads, (Z, 1)), "z", split_axis=0, concat_axis=0, tiled=True)
    grads = jnp.sum(by_z.reshape(Z, EXTRA, HIDDEN).astype(f32), axis=0)
    grads = grads + 0.0 * third
    grad_w = lax.all_to_all(
        jnp.tile(grads[:GRAD_ROWS], (N_BLK, 1)), BLK, split_axis=0, concat_axis=0, tiled=True
    )
    return (activated, grad_x.reshape(NB, HIDDEN), grad_w, grads[GRAD_ROWS])


def solution(mesh):
    cut = Mesh(mesh.devices.reshape(XH, Z, CORE, Y, XL), AXES)
    row = ("xh", "z", "core")
    return jax.shard_map(
        shards,
        mesh=cut,
        in_specs=(
            P(AXES, None),
            P(row, BLK, None, None),
            P(row, BLK),
            P(row, BLK),
            P(),
            P(),
            P(AXES, None),
        ),
        out_specs=(P(AXES, None), P(AXES, None), P(), P()),
        check_vma=False,
    )
```

```python
import functools
import math

import jax
import jax.numpy as jnp
from jax import lax
from jax.experimental import pallas as pl
from jax.experimental.pallas import tpu as pltpu
from jax.sharding import Mesh, PartitionSpec as P

XH, Z, CORE, Y, XL = 2, 8, 2, 4, 2
AXES = ("xh", "z", "core", "y", "xl")
BLK = ("y", "xl")
N_BLK = Y * XL
TILE = 128
HIDDEN = 256
PER = 3
NB = PER * TILE
TR = N_BLK * PER
TC = XH * Z * CORE * PER
K = 288
GROUP = 16
GROUPS = K // GROUP
EXTRA = 48
GRAD_ROWS = HIDDEN // N_BLK
CHAIN = Z // 2 * XH * PER
VMEM_BYTES = 56 * 2**20
bf16 = jnp.bfloat16
f32 = jnp.float32

TILE_COST = pl.CostEstimate(
    flops=2 * K * TILE * TILE * HIDDEN, bytes_accessed=6 * K * TILE * TILE, transcendentals=0
)
ANY = pl.BlockSpec(memory_space=pl.ANY)
VMEM = pl.BlockSpec(memory_space=pltpu.VMEM)


def swap(axis):
    return lambda v: lax.ppermute(v, axis, [(0, 1), (1, 0)])


def turn(v, step):
    return lax.ppermute(v, "z", [(i, (i + step) % Z) for i in range(Z)])


def fetch_group(live, adj_hbm, adj, sem, g):
    first = jnp.minimum(g * GROUP, K - GROUP)
    return pltpu.make_async_copy(adj_hbm.at[pl.ds(first, GROUP)], adj.at[g], sem.at[g])


def start_groups(live_ref, adj_hbm, adj, sem):
    live = live_ref[0]
    groups = (live + GROUP - 1) // GROUP

    def begin(g, carry):
        fetch_group(live, adj_hbm, adj, sem, g).start()
        return carry

    lax.fori_loop(0, groups, begin, 0)
    return live, groups


def forward_kernel(live_ref, row_ref, pos_ref, adj_hbm, *refs):
    pieces = refs[:-6]
    out_ref, adj, slab, acc, adj_sem, piece_sem = refs[-6:]
    copies = []
    at = 0
    for n, piece in enumerate(pieces):
        size = piece.shape[0]
        copies.append(pltpu.make_async_copy(piece, slab.at[pl.ds(at, size)], piece_sem.at[n]))
        at += size
    for copy in copies:
        copy.start()
    live, groups = start_groups(live_ref, adj_hbm, adj, adj_sem)
    acc[...] = jnp.zeros_like(acc)
    for copy in copies:
        copy.wait()

    def step(g, carry):
        fetch_group(live, adj_hbm, adj, adj_sem, g).wait()
        for u in range(GROUP):
            k = g * GROUP + u
            row = jnp.where(k < live, row_ref[k], TR)
            acc[row] += jnp.dot(adj[g, u], slab[pos_ref[k]], preferred_element_type=f32)
        return carry

    lax.fori_loop(0, groups, step, 0)
    out_ref[...] = acc[:TR].astype(bf16)


def forward_tiles(live, rows, pos, adj, pieces):
    return pl.pallas_call(
        forward_kernel,
        out_shape=jax.ShapeDtypeStruct((TR, TILE, HIDDEN), bf16),
        grid_spec=pltpu.PrefetchScalarGridSpec(
            num_scalar_prefetch=3,
            grid=(),
            in_specs=[ANY] * (1 + len(pieces)),
            out_specs=VMEM,
            scratch_shapes=[
                pltpu.VMEM((GROUPS, GROUP, TILE, TILE), bf16),
                pltpu.VMEM((TC, TILE, HIDDEN), bf16),
                pltpu.VMEM((TR + 1, TILE, HIDDEN), f32),
                pltpu.SemaphoreType.DMA((GROUPS,)),
                pltpu.SemaphoreType.DMA((len(pieces),)),
            ],
        ),
        compiler_params=pltpu.CompilerParams(vmem_limit_bytes=VMEM_BYTES),
        cost_estimate=TILE_COST,
        name="forward_tiles",
    )(live, rows, pos, adj, *pieces)


def backward_kernel(live_ref, row_ref, pos_ref, adj_hbm, err_hbm, *refs):
    outs = refs[:-5]
    adj, err, acc, adj_sem, err_sem = refs[-5:]
    copies = [
        pltpu.make_async_copy(
            err_hbm.at[i // PER, pl.ds(i % PER * TILE, TILE)], err.at[i], err_sem.at[i]
        )
        for i in range(TR)
    ]
    for copy in copies:
        copy.start()
    live, groups = start_groups(live_ref, adj_hbm, adj, adj_sem)
    acc[...] = jnp.zeros_like(acc)
    for copy in copies:
        copy.wait()

    def step(g, carry):
        fetch_group(live, adj_hbm, adj, adj_sem, g).wait()
        for u in range(GROUP):
            k = g * GROUP + u
            pos = jnp.where(k < live, pos_ref[k], TC)
            acc[pos] += lax.dot_general(
                adj[g, u], err[row_ref[k]], (((0,), (0,)), ((), ())), preferred_element_type=f32
            )
        return carry

    lax.fori_loop(0, groups, step, 0)
    at = 0
    for out in outs:
        out[...] = acc[at : at + out.shape[0]].astype(bf16)
        at += out.shape[0]


def backward_tiles(live, rows, pos, adj, err):
    return pl.pallas_call(
        backward_kernel,
        out_shape=[jax.ShapeDtypeStruct((XH * PER, TILE, HIDDEN), bf16)] * Z
        + [jax.ShapeDtypeStruct((CHAIN, TILE, HIDDEN), bf16)] * 2,
        grid_spec=pltpu.PrefetchScalarGridSpec(
            num_scalar_prefetch=3,
            grid=(),
            in_specs=[ANY, ANY],
            out_specs=[VMEM] * (Z + 2),
            scratch_shapes=[
                pltpu.VMEM((GROUPS, GROUP, TILE, TILE), bf16),
                pltpu.VMEM((TR, TILE, HIDDEN), bf16),
                pltpu.VMEM((TC + 1, TILE, HIDDEN), f32),
                pltpu.SemaphoreType.DMA((GROUPS,)),
                pltpu.SemaphoreType.DMA((TR,)),
            ],
        ),
        compiler_params=pltpu.CompilerParams(vmem_limit_bytes=VMEM_BYTES),
        cost_estimate=TILE_COST,
        name="backward_tiles",
    )(live, rows, pos, adj, err)


def dense_kernel(scale, parts_ref, weight_ref, bias_ref, cot_ref, act_ref, back_ref):
    summed = parts_ref[0].astype(f32)
    for b in range(1, N_BLK):
        summed = summed + parts_ref[b].astype(f32)
    agg = summed.astype(bf16)
    weight = weight_ref[...]
    v = jnp.dot(agg, weight, preferred_element_type=f32) + bias_ref[...]
    c = math.sqrt(2.0 / math.pi)
    t = jnp.tanh(c * (v + 0.044715 * (v * v * v)))
    act_ref[...] = (0.5 * v * (1.0 + t)).astype(bf16)
    slope = 0.5 * (1.0 + t) + 0.5 * v * (1.0 - t * t) * (c * (1.0 + 3.0 * 0.044715 * (v * v)))
    delta = (cot_ref[...].astype(f32) * slope).astype(bf16)
    back = lax.dot_general(
        delta, weight, (((1,), (1,)), ((), ())), preferred_element_type=f32
    ).astype(bf16)
    over_nodes = (((0,), (0,)), ((), ()))
    grad_w = lax.dot_general(agg, delta, over_nodes, preferred_element_type=f32) * scale
    grad_b = jnp.sum(delta.astype(f32), axis=0, keepdims=True) * scale
    grad_b = jnp.broadcast_to(grad_b, (EXTRA - GRAD_ROWS, HIDDEN)).astype(bf16)
    for b in range(N_BLK):
        back_ref[b, :NB] = back
        back_ref[b, NB : NB + GRAD_ROWS] = grad_w[b * GRAD_ROWS : (b + 1) * GRAD_ROWS].astype(bf16)
        back_ref[b, NB + GRAD_ROWS :] = grad_b


def dense_block(parts, weight, bias, cot, scale):
    return pl.pallas_call(
        functools.partial(dense_kernel, scale),
        out_shape=[
            jax.ShapeDtypeStruct((NB, HIDDEN), bf16),
            jax.ShapeDtypeStruct((N_BLK, NB + EXTRA, HIDDEN), bf16),
        ],
        in_specs=[VMEM] * 4,
        out_specs=[VMEM] * 2,
        compiler_params=pltpu.CompilerParams(vmem_limit_bytes=VMEM_BYTES),
        name="dense_block",
    )(parts, weight, bias, cot)


def gather_pieces(own):
    here, across = own, swap("xh")(own)
    near = [(here, across)]
    right = left = near[0]
    for _ in range(3):
        right = tuple(turn(v, 1) for v in right)
        left = tuple(turn(v, -1) for v in left)
        near += [right, left]
    near.append((turn(right[0], 1), turn(left[1], -1)))
    pieces = []
    for pair in near:
        pieces += [*pair, *(swap("core")(v) for v in pair)]
    return pieces


def place_of(cols, xh, z, core):
    owner = cols // PER
    away = ((owner // CORE) % Z - z) % Z
    near = jnp.where(away <= 3, 2 * away, 15 - 2 * away)
    return near, (owner % CORE) ^ core, (owner // (CORE * Z)) ^ xh, cols % PER


def scatter_sum(keep, sends):
    odd = swap("core")(sends[1])
    received = [swap("core")(sends[0]), odd]

    def mine(near):
        at = slice(near // 2 * XH * PER, (near // 2 + 1) * XH * PER)
        return keep[near].astype(f32) + received[near % 2][at].astype(f32)

    far = mine(7).astype(bf16)
    right, left = turn(far[:PER], 1), turn(far[PER:], -1)
    first = right[0, :EXTRA].astype(f32) + left[0, :EXTRA].astype(f32)
    onto_right, onto_left = mine(6), mine(5)
    right = jnp.concatenate([onto_right[:PER] + right.astype(f32), onto_right[PER:]], axis=0)
    left = jnp.concatenate([onto_left[:PER], onto_left[PER:] + left.astype(f32)], axis=0)
    for near in (4, 2):
        right, left = turn(right.astype(bf16), 1), turn(left.astype(bf16), -1)
        third = right[0, :EXTRA].astype(f32) + left[0, :EXTRA].astype(f32)
        right = mine(near) + right.astype(f32)
        left = mine(near - 1) + left.astype(f32)
    here = mine(0) + turn(right.astype(bf16), 1).astype(f32) + turn(left.astype(bf16), -1).astype(f32)
    across = swap("xh")(here[PER:].astype(bf16))
    return (here[:PER] + across.astype(f32)).astype(bf16), first, third


def both_sides(rows, axis):
    rows = rows.astype(bf16)
    return rows.astype(f32) + swap(axis)(rows).astype(f32)


def shards(features, adj_tiles, tile_row, tile_col, weight, bias_vec, cotangent):
    adj = adj_tiles[0]
    rows = tile_row[0]
    cols = tile_col[0]
    xh, z, core = (lax.axis_index(axis) for axis in ("xh", "z", "core"))
    live = jnp.sum((cols < TC).astype(jnp.int32)).reshape(1)
    near, other, across, part = place_of(jnp.minimum(cols, TC - 1), xh, z, core)
    slab_pos = ((near * CORE + other) * XH + across) * PER + part
    place = jnp.where(other == 0, near, Z + near % 2 * (Z // 2) + near // 2)
    sum_pos = (place * XH + across) * PER + part

    pieces = gather_pieces(features.reshape(PER, TILE, HIDDEN))
    partial = forward_tiles(live, rows, slab_pos, adj, pieces)
    parts = lax.all_to_all(
        partial.reshape(N_BLK, NB, HIDDEN), BLK, split_axis=0, concat_axis=0, tiled=True
    )
    scale = 1.0 / math.sqrt(NB * XH * Z * CORE * N_BLK)
    activated, back = dense_block(parts, weight, bias_vec.reshape(1, HIDDEN), cotangent, scale)
    back = lax.all_to_all(back, BLK, split_axis=0, concat_axis=0, tiled=True)

    outs = backward_tiles(live, rows, sum_pos, adj, back)
    grad_x, first, third = scatter_sum(outs[:Z], outs[Z:])

    grads = jnp.sum(back[:, NB:].astype(f32), axis=0)
    grads = both_sides(both_sides(grads, "core"), "xh")
    grads = (grads + 0.0 * first).astype(bf16)
    by_z = lax.all_to_all(jnp.tile(grads, (Z, 1)), "z", split_axis=0, concat_axis=0, tiled=True)
    grads = jnp.sum(by_z.reshape(Z, EXTRA, HIDDEN).astype(f32), axis=0)
    grads = grads + 0.0 * third
    grad_w = lax.all_to_all(
        jnp.tile(grads[:GRAD_ROWS], (N_BLK, 1)), BLK, split_axis=0, concat_axis=0, tiled=True
    )
    return (activated, grad_x.reshape(NB, HIDDEN), grad_w, grads[GRAD_ROWS])


def solution(mesh):
    cut = Mesh(mesh.devices.reshape(XH, Z, CORE, Y, XL), AXES)
    row = ("xh", "z", "core")
    return jax.shard_map(
        shards,
        mesh=cut,
        in_specs=(
            P(AXES, None),
            P(row, BLK, None, None),
            P(row, BLK),
            P(row, BLK),
            P(),
            P(),
            P(AXES, None),
        ),
        out_specs=(P(AXES, None), P(AXES, None), P(), P()),
        check_vma=False,
    )
```
